32 devices in a mesh: grp: 2 (over y), mk: 4 (over z), pp: 2 (over x), sub: 2 (over core).
Axes of the slice: x: 2, y: 2, z: 4, core: 2. Of those that a mesh axis runs over, the one named last changes fastest.
Arguments:
- genotypes: bfloat16 [4096, 16384], P(('grp', 'pp', 'sub'), 'mk'), parts along dimension 0, may hold values from -6 to 6
- estimate: bfloat16 [512, 16384], P(('grp', 'pp', 'sub'), 'mk'), parts along dimension 0, may hold values from -0.046875 to 0.046875
- phenotypes: bfloat16 [512, 2048], P('grp', ('pp', 'sub')), parts along dimension 0, may hold values from -6 to 6
- prior_logit: float32 [512], P(('grp', 'pp', 'sub')), parts along dimension 0, may hold values from -2 to 1
- slab_var: float32 [512], P(('grp', 'pp', 'sub')), parts along dimension 0, may hold values from 0.5 to 4
- noise_var: float32 [512], P(('grp', 'pp', 'sub')), parts along dimension 0, may hold values from 0.5 to 2
- tile_chrom: int32 [64], P('grp'), parts along dimension 0, may hold values from 0 to 21, as said below
Outputs:
- updated: bfloat16 [512, 16384], P(('grp', 'pp', 'sub'), 'mk'), parts along dimension 0
- loco_out: bfloat16 [44, 256, 2048], P('grp', 'mk', ('pp', 'sub')), parts along dimension 0
The draws below stay inside these ranges and needn't reach their ends.
There are 2 independent parts, one for each index of `grp`. The reference program is written for one: setup_inputs(seed, part) draws one part's arguments, and reference() takes and returns one part's arrays. A program takes and returns all parts, laid end to end along the dimension named above; each array names one. Nothing has to cross between parts.
Inputs may be any that keep to these rules, and one draw needn't show every extreme that they name: `tile_chrom`: never falling along the tiles; every chromosome owns at least one tile; the tiles of one device (aligned blocks of 8 tiles) name at most 6 chromosomes, and some device names exactly 6.
All inputs are finite; a program needn't handle non-finite values.
Results may differ from the reference program's by a relative error of at most 0.0059.
Values may be sent and summed in bfloat16 or wider, within the bound.
No kernel may reach another device: no remote copies, remote signals or barrier semaphores. Data moves between devices by JAX's collectives and lax.ppermute only.
A program may use at most 64 MiB of HBM per device.

```python
import math
import jax
import jax.numpy as jnp
from jax import lax

TRAITS = 256
CHROMS = 22
TILE = 512
SPAN = 6
MARK_DEV = 4096
PEOPLE = 2048
MARKERS = 16384
TILES = 32
N_MK = 4


def draw_tile_chrom(key, part):
    tile_dev = MARK_DEV // TILE
    place_count = TILES - 1
    subkeys = jax.random.split(key, 2)
    scores = jax.random.permutation(subkeys[0], place_count).astype(jnp.int32)
    places = jnp.arange(1, TILES, dtype=jnp.int32)
    owners = places // tile_dev
    inside = places % tile_dev != 0
    same_dev = (owners[:, None] == owners[None, :]) & inside[None, :] & inside[:, None]
    higher = jnp.sum((same_dev & (scores[None, :] > scores[:, None])).astype(jnp.int32), axis=1)
    allowed = jnp.logical_not(inside) | (higher < SPAN - 1)
    chosen_dev = jax.random.randint(subkeys[1], (), 0, N_MK).astype(jnp.int32)
    forced = inside & (owners == chosen_dev) & (higher < SPAN - 1)
    priority = jnp.where(forced, scores + 2 * TILES, jnp.where(allowed, scores, -TILES - places))
    top_values, picked = lax.top_k(priority, CHROMS - 1)
    increments = jnp.zeros((place_count,), jnp.int32).at[picked].set(1)
    return jnp.concatenate([jnp.zeros((1,), jnp.int32), jnp.cumsum(increments).astype(jnp.int32)])


def block_scale(key, shape, cuts, least, high):
    level, own = 1.0, jax.random.fold_in(key, 6)
    for axis_at, shards_of in cuts:
        heights = jnp.exp(jax.random.uniform(jax.random.fold_in(own, axis_at), (shards_of,), jnp.float32, least / len(cuts), high / len(cuts)))
        level = level * jnp.repeat(heights, shape[axis_at] // shards_of).reshape([-1 if axis == axis_at else 1 for axis in range(len(shape))])
    return level


def normal_values(stream_key, extent, scale, limit, shards=(), kind=jnp.bfloat16):
    level = block_scale(stream_key, extent, shards, -0.22, 0.18) if shards else 1.0
    drawn = jax.random.normal(stream_key, extent, jnp.float32) * scale * level
    return jnp.minimum(jnp.maximum(drawn, -limit), limit).astype(kind)


def setup_inputs(seed: int = 0, part: int = 0) -> dict:
    keys = jax.random.split(jax.random.key(seed), 8)
    part_splits = jax.random.split(jax.random.fold_in(keys[7], part), 8)
    return {
        "genotypes": normal_values(part_splits[0], (PEOPLE, MARKERS), 1.0, 6.0, ((0, 4), (1, 4))),
        "estimate": normal_values(part_splits[1], (TRAITS, MARKERS), MARKERS ** -0.5, 0.046875, ((0, 4), (1, 4))),
        "phenotypes": normal_values(part_splits[2], (TRAITS, PEOPLE), 1.0, 6.0, ((1, 4),)),
        "prior_logit": jnp.clip(-2.0 + 3.0 * jax.random.uniform(part_splits[3], (TRAITS,), jnp.float32) ** block_scale(part_splits[3], (TRAITS,), ((0, 4),), -0.2, 0.2), -2.0, 1.0),
        "slab_var": jnp.clip(jnp.exp(math.log(4.0) - 2.0794415 * jax.random.uniform(part_splits[4], (TRAITS,), jnp.float32) ** block_scale(part_splits[4], (TRAITS,), ((0, 4),), -0.2, 0.2)), 0.5, 4.0),
        "noise_var": jnp.clip(jnp.exp(math.log(2.0) - 1.3862944 * jax.random.uniform(part_splits[5], (TRAITS,), jnp.float32) ** block_scale(part_splits[5], (TRAITS,), ((0, 4),), -0.2, 0.2)), 0.5, 2.0),
        "tile_chrom": draw_tile_chrom(jax.random.fold_in(jax.random.fold_in(keys[7], part), 71), part),
    }


def denoise(estimate, scores, prior_logit, slab_var, noise_var, marker_root, people_root):
    observed = marker_root * estimate.astype(jnp.float32) + scores * (1.0 / people_root)
    slab_col = slab_var[:, None]
    noise_col = noise_var[:, None]
    spread = slab_col + noise_col
    log_odds = prior_logit[:, None] + 0.5 * jnp.log(noise_col / spread) + 0.5 * observed * observed * (1.0 / noise_col - 1.0 / spread)
    posterior = jax.nn.sigmoid(log_odds) * (slab_col / spread) * observed
    return (posterior * (1.0 / marker_root)).astype(jnp.bfloat16)

def reference(genotypes, estimate, phenotypes, prior_logit, slab_var, noise_var, tile_chrom):
    prediction = lax.dot_general(estimate, genotypes, (((1,), (1,)), ((), ())), preferred_element_type=jnp.float32)
    residual = (phenotypes.astype(jnp.float32) - prediction).astype(jnp.bfloat16)
    scores = jnp.dot(residual, genotypes, preferred_element_type=jnp.float32)
    updated = denoise(estimate, scores, prior_logit, slab_var, noise_var, math.sqrt(MARKERS), math.sqrt(PEOPLE))

    def add_tile(tile_index, buffer):
        where_at = (tile_index * TILE).astype(jnp.int32)
        geno_tile = lax.dynamic_slice_in_dim(genotypes, where_at, TILE, 1)
        est_tile = lax.dynamic_slice_in_dim(updated, where_at, TILE, 1)
        product = lax.dot_general(est_tile, geno_tile, (((1,), (1,)), ((), ())), preferred_element_type=jnp.float32)
        chrom_id = lax.dynamic_index_in_dim(tile_chrom, tile_index.astype(jnp.int32), 0, keepdims=False).astype(jnp.int32)
        old_row = lax.dynamic_index_in_dim(buffer, chrom_id, 0, keepdims=False)
        return lax.dynamic_update_index_in_dim(buffer, old_row + product, chrom_id, 0)
    chrom_sums = lax.fori_loop(0, TILES, add_tile, jnp.zeros((CHROMS, TRAITS, PEOPLE), jnp.float32))
    combined = lax.optimization_barrier(jnp.sum(chrom_sums, axis=0))
    loco_out = (phenotypes.astype(jnp.float32)[None] - combined[None] + chrom_sums).astype(jnp.bfloat16)
    return (updated, loco_out)
```

```python
import functools
import math

import jax
import jax.numpy as jnp
from jax import lax
from jax.experimental import pallas as pl
from jax.experimental.pallas import tpu as pltpu
from jax.sharding import PartitionSpec as P

CHROMS = 22
TILE = 512
SPAN = 6
PIECES = 4


def denoise(estimate, scores, prior_logit, slab_var, noise_var, marker_root, people_root):
    observed = marker_root * estimate.astype(jnp.float32) + scores * (1.0 / people_root)
    slab_col = slab_var[:, None]
    noise_col = noise_var[:, None]
    spread = slab_col + noise_col
    log_odds = (
        prior_logit[:, None]
        + 0.5 * jnp.log(noise_col / spread)
        + 0.5 * observed * observed * (1.0 / noise_col - 1.0 / spread)
    )
    posterior = jax.nn.sigmoid(log_odds) * (slab_col / spread) * observed
    return (posterior * (1.0 / marker_root)).astype(jnp.bfloat16)


def whole_mesh_steps(genotypes, estimate, phenotypes, prior_logit, slab_var, noise_var, tile_chrom):
    people_dev, mark_dev = genotypes.shape
    mk_count = lax.axis_size("mk")
    people_count = lax.axis_size(("pp", "sub"))
    traits = phenotypes.shape[0]
    partial_pred = lax.dot_general(
        lax.all_gather(estimate, ("pp", "sub"), axis=0, tiled=True),
        genotypes,
        (((1,), (1,)), ((), ())),
        preferred_element_type=jnp.float32,
    )
    share_rows = traits // mk_count
    offset = lax.axis_index("mk") * share_rows
    phen_share = lax.dynamic_slice_in_dim(phenotypes, offset, share_rows, 0).astype(jnp.float32)
    prediction = lax.psum(partial_pred, "mk")
    residual = (phenotypes.astype(jnp.float32) - prediction).astype(jnp.bfloat16)
    scores = lax.psum_scatter(
        jnp.dot(residual, genotypes, preferred_element_type=jnp.float32),
        ("pp", "sub"),
        scatter_dimension=0,
        tiled=True,
    )
    updated = denoise(
        estimate,
        scores,
        prior_logit,
        slab_var,
        noise_var,
        math.sqrt(mark_dev * mk_count),
        math.sqrt(people_dev * people_count),
    )
    tile_dev = mark_dev // TILE
    own_tiles = lax.dynamic_slice_in_dim(tile_chrom, lax.axis_index("mk") * tile_dev, tile_dev, 0)
    labels = own_tiles[0] + jnp.arange(SPAN, dtype=jnp.int32)
    member = (labels[:, None] == own_tiles[None, :]).astype(jnp.float32)
    geno_tiles = genotypes.reshape(people_dev, tile_dev, TILE)
    shard_rows = lax.all_gather(updated, ("pp", "sub"), axis=0, tiled=True)
    tile_terms = jnp.einsum(
        "kta,pta->tkp",
        shard_rows.reshape(shard_rows.shape[0], tile_dev, TILE),
        geno_tiles,
        preferred_element_type=jnp.float32,
    )
    local_sums = jnp.einsum("st,tkp->skp", member, tile_terms, precision=lax.Precision.HIGHEST)
    received = lax.all_to_all(local_sums, "mk", split_axis=1, concat_axis=0, tiled=True)
    firsts = tile_chrom.reshape(mk_count, tile_dev)[:, 0]
    sources = (firsts[:, None] + jnp.arange(SPAN, dtype=jnp.int32)[None, :]).reshape(-1)
    assign = (jnp.arange(CHROMS, dtype=jnp.int32)[:, None] == sources[None, :]).astype(jnp.float32)
    chrom_sums = jnp.einsum("cj,jkp->ckp", assign, received, precision=lax.Precision.HIGHEST)
    combined = jnp.sum(chrom_sums, axis=0)
    loco_out = (phen_share[None] - combined[None] + chrom_sums).astype(jnp.bfloat16)
    return (updated, loco_out)


VMEM = pltpu.MemorySpace.VMEM
NT = (((1,), (1,)), ((), ()))


def local_call(body, outs, args, scalars=(), scratch=(), flops=0):
    in_bytes = sum(a.size * a.dtype.itemsize for a in args)
    out_bytes = sum(math.prod(s) * jnp.dtype(d).itemsize for s, d in outs)
    return pl.pallas_call(
        body,
        out_shape=[pltpu.VMEM(s, d) for s, d in outs],
        in_specs=[pl.BlockSpec(memory_space=pltpu.SMEM)] * len(scalars)
        + [pl.BlockSpec(memory_space=VMEM)] * len(args),
        out_specs=[pl.BlockSpec(memory_space=VMEM)] * len(outs),
        scratch_shapes=list(scratch),
        cost_estimate=pl.CostEstimate(flops=flops, bytes_accessed=in_bytes + out_bytes, transcendentals=0),
        compiler_params=pltpu.CompilerParams(vmem_limit_bytes=8 * 2**20),
    )(*scalars, *[pltpu.with_memory_space_constraint(a, VMEM) for a in args])


def predict_body(where, own, across, beside, geno, keep, send):
    odd = where[0]
    half = 2 * own.shape[0]
    rows = jnp.concatenate([own[...], across[...], beside[...]], axis=0)
    product = lax.dot_general(rows, geno[...], NT, preferred_element_type=jnp.float32)

    @pl.when(odd == 0)
    def _():
        keep[...] = product[:half]
        send[...] = product[half:].astype(send.dtype)

    @pl.when(odd == 1)
    def _():
        keep[...] = product[half:]
        send[...] = product[:half].astype(send.dtype)


def score_body(where, mine, other, geno, keep, send):
    even = where[0] == 0
    half = mine.shape[0]
    first = jnp.where(even, mine[...], other[...])
    second = jnp.where(even, other[...], mine[...])
    rows = jnp.concatenate([first, second], axis=0)
    width = 512
    for at in range(0, geno.shape[1], width):
        product = jnp.dot(rows, geno[:, at : at + width], preferred_element_type=jnp.float32)
        keep[:, at : at + width] = product[:half]
        send[:, at : at + width] = product[half:].astype(send.dtype)


def chrom_body(where, labels, own, beside, geno, *outs_and_acc):
    *outs, acc = outs_and_acc
    height = own.shape[0] // 2
    tiles = labels.shape[0]
    for out in outs:
        out[...] = jnp.zeros_like(out)
    for tile in range(tiles):
        columns = slice(tile * TILE, (tile + 1) * TILE)
        rows = jnp.concatenate([own[:, columns], beside[:, columns]], axis=0)
        product = lax.dot_general(rows, geno[:, columns], NT, preferred_element_type=jnp.float32)
        if tile == 0:
            acc[...] = product
        else:
            same = (labels[tile] == labels[tile - 1]).astype(jnp.float32)
            acc[...] = acc[...] * same + product
        slot = labels[tile] - labels[0]
        for to, out in enumerate(outs):
            start = pl.multiple_of(where[1 + to] * height, height)
            out[slot] = acc[pl.ds(start, height), :].astype(out.dtype)


def loco_body(firsts, phen, *refs):
    *sums, out, base, acc = refs
    total = jnp.zeros(base.shape, jnp.float32)
    for part in sums:
        for slot in range(SPAN):
            total = total + part[slot].astype(jnp.float32)
    base[...] = phen[...].astype(jnp.float32) - total

    def step(chrom, carry):
        acc[...] = base[...]
        for at, part in enumerate(sums):
            slot = chrom - firsts[at]

            @pl.when((slot >= 0) & (slot < SPAN))
            def _():
                acc[...] += part[slot].astype(jnp.float32)

        out[chrom] = acc[...].astype(out.dtype)
        return carry

    lax.fori_loop(0, CHROMS, step, 0)


def piece_steps(genotypes, estimate, phenotypes, prior_logit, slab_var, noise_var, tile_chrom):
    people_dev, mark_dev = genotypes.shape
    shard = estimate.shape[0]
    mk_count = lax.axis_size("mk")
    people_count = lax.axis_size(("pp", "sub"))
    marker_root = math.sqrt(mark_dev * mk_count)
    people_root = math.sqrt(people_dev * people_count)
    tile_dev = mark_dev // TILE
    me = lax.axis_index("pp") * 2 + lax.axis_index("sub")
    depth = lax.axis_index("mk")
    odd = depth % 2
    swap = [(0, 1), (1, 0)]

    def along(step):
        return [(i, i ^ step) for i in range(mk_count)]

    def block_for(step):
        bits = me ^ depth ^ step
        return (bits % 2) * 2 + bits // 2

    where = jnp.stack([odd] + [block_for(step) for step in range(mk_count)]).astype(jnp.int32)
    labels = lax.dynamic_slice_in_dim(tile_chrom, depth * tile_dev, tile_dev, 0)
    all_firsts = tile_chrom.reshape(mk_count, tile_dev)[:, 0]
    firsts = jnp.stack([all_firsts[depth ^ step] for step in range(mk_count)])
    phen_one = lax.dynamic_slice_in_dim(phenotypes, (me ^ odd) * shard, shard, 0)
    phen_two = lax.dynamic_slice_in_dim(phenotypes, (me ^ odd ^ 2) * shard, shard, 0)
    phen_share = lax.dynamic_slice_in_dim(phenotypes, depth * shard, shard, 0)
    params = jnp.stack([prior_logit, slab_var, noise_var])
    params_across = lax.ppermute(params, "pp", swap)

    (geno,) = local_call(
        lambda source, target: target.__setitem__(..., source[...]),
        [(genotypes.shape, genotypes.dtype)],
        [genotypes],
    )
    height = shard // PIECES
    traits = 4 * height
    updates, locos = [], []
    for piece in range(PIECES):
        rows = slice(piece * height, (piece + 1) * height)
        own = estimate[rows]
        across = lax.ppermute(own, "pp", swap)
        pair = jnp.concatenate([own, across], axis=0)
        beside = lax.ppermute(pair, "sub", swap)
        matmul = 2 * traits * people_dev * mark_dev
        half = (2 * height, people_dev)
        keep, send = local_call(
            predict_body, [(half, jnp.float32), (half, jnp.bfloat16)], [own, across, beside, geno], [where], flops=matmul
        )
        two = (keep + lax.ppermute(send, "mk", along(1)).astype(jnp.float32)).astype(jnp.bfloat16)
        four = two.astype(jnp.float32) + lax.ppermute(two, "mk", along(2)).astype(jnp.float32)
        phen = jnp.concatenate([phen_one[rows], phen_two[rows]], axis=0).astype(jnp.float32)
        residual = (phen - four).astype(jnp.bfloat16)
        residual_other = lax.ppermute(residual, "mk", along(1))
        wide = (2 * height, mark_dev)
        keep, send = local_call(
            score_body, [(wide, jnp.float32), (wide, jnp.bfloat16)], [residual, residual_other, geno], [where], flops=matmul
        )
        chip = keep + lax.ppermute(send, "sub", swap).astype(jnp.float32)
        chip_across = jnp.concatenate([chip[height:], chip[:height]], axis=0).astype(jnp.bfloat16)
        scores = chip + lax.ppermute(chip_across, "pp", swap).astype(jnp.float32)
        pair_params = jnp.concatenate([params[:, rows], params_across[:, rows]], axis=1)
        updated = denoise(pair, scores, *pair_params, marker_root, people_root)
        updates.append(updated[:height])
        updated_beside = lax.ppermute(updated, "sub", swap)
        block = ((SPAN, height, people_dev), jnp.bfloat16)
        sums = local_call(
            chrom_body,
            [block] * mk_count,
            [updated, updated_beside, geno],
            [where, labels],
            scratch=[pltpu.VMEM((traits, people_dev), jnp.float32)],
            flops=matmul,
        )
        got = [sums[0]] + [lax.ppermute(sums[step], "mk", along(step)) for step in range(1, mk_count)]
        (loco,) = local_call(
            loco_body,
            [((CHROMS, height, people_dev), jnp.bfloat16)],
            [phen_share[rows], *got],
            [firsts],
            scratch=[pltpu.VMEM((height, people_dev), jnp.float32)] * 2,
            flops=10 * CHROMS * height * people_dev,
        )
        locos.append(loco)
    return (jnp.concatenate(updates, axis=0), jnp.concatenate(locos, axis=1))


def solution(mesh):
    placed = (
        P(("grp", "pp", "sub"), "mk"),
        P(("grp", "pp", "sub"), "mk"),
        P("grp", ("pp", "sub")),
        P(("grp", "pp", "sub")),
        P(("grp", "pp", "sub")),
        P(("grp", "pp", "sub")),
        P("grp"),
    )
    by_pieces = (mesh.shape["pp"], mesh.shape["sub"], mesh.shape["mk"]) == (2, 2, 4)
    return jax.shard_map(
        piece_steps if by_pieces else whole_mesh_steps,
        mesh=mesh,
        in_specs=placed,
        out_specs=(P(("grp", "pp", "sub"), "mk"), P("grp", "mk", ("pp", "sub"))),
        check_vma=False,
    )
```

```python
import functools
import math

import jax
import jax.numpy as jnp
from jax import lax
from jax.experimental import pallas as pl
from jax.experimental.pallas import tpu as pltpu
from jax.sharding import PartitionSpec as P

CHROMS = 22
TILE = 512
SPAN = 6
LOADS = 2
SPLIT = 4
CHAIN = True
FIRST = (1, 1)
SECOND = ((0, 0, 1, 1), (1, 0, 1, 1))
ORDER = (('pred', 0), ('two', 0), ('pred', 1), ('res', 0), ('two', 1), ('score', 0), ('chip', 0), ('res', 1), ('score', 1), ('chip', 1), ('den', 0), ('chrom', 0), ('den', 1), ('chrom', 1), ('leave', 0), ('leave', 1))


def denoise(estimate, scores, prior_logit, slab_var, noise_var, marker_root, people_root):
    observed = marker_root * estimate.astype(jnp.float32) + scores * (1.0 / people_root)
    slab_col = slab_var[:, None]
    noise_col = noise_var[:, None]
    spread = slab_col + noise_col
    log_odds = (
        prior_logit[:, None]
        + 0.5 * jnp.log(noise_col / spread)
        + 0.5 * observed * observed * (1.0 / noise_col - 1.0 / spread)
    )
    posterior = jax.nn.sigmoid(log_odds) * (slab_col / spread) * observed
    return (posterior * (1.0 / marker_root)).astype(jnp.bfloat16)


def whole_mesh_steps(genotypes, estimate, phenotypes, prior_logit, slab_var, noise_var, tile_chrom):
    people_dev, mark_dev = genotypes.shape
    mk_count = lax.axis_size("mk")
    people_count = lax.axis_size(("pp", "sub"))
    traits = phenotypes.shape[0]
    partial_pred = lax.dot_general(
        lax.all_gather(estimate, ("pp", "sub"), axis=0, tiled=True),
        genotypes,
        (((1,), (1,)), ((), ())),
        preferred_element_type=jnp.float32,
    )
    share_rows = traits // mk_count
    offset = lax.axis_index("mk") * share_rows
    phen_share = lax.dynamic_slice_in_dim(phenotypes, offset, share_rows, 0).astype(jnp.float32)
    prediction = lax.psum(partial_pred, "mk")
    residual = (phenotypes.astype(jnp.float32) - prediction).astype(jnp.bfloat16)
    scores = lax.psum_scatter(
        jnp.dot(residual, genotypes, preferred_element_type=jnp.float32),
        ("pp", "sub"),
        scatter_dimension=0,
        tiled=True,
    )
    updated = denoise(
        estimate,
        scores,
        prior_logit,
        slab_var,
        noise_var,
        math.sqrt(mark_dev * mk_count),
        math.sqrt(people_dev * people_count),
    )
    tile_dev = mark_dev // TILE
    own_tiles = lax.dynamic_slice_in_dim(tile_chrom, lax.axis_index("mk") * tile_dev, tile_dev, 0)
    labels = own_tiles[0] + jnp.arange(SPAN, dtype=jnp.int32)
    member = (labels[:, None] == own_tiles[None, :]).astype(jnp.float32)
    geno_tiles = genotypes.reshape(people_dev, tile_dev, TILE)
    shard_rows = lax.all_gather(updated, ("pp", "sub"), axis=0, tiled=True)
    tile_terms = jnp.einsum(
        "kta,pta->tkp",
        shard_rows.reshape(shard_rows.shape[0], tile_dev, TILE),
        geno_tiles,
        preferred_element_type=jnp.float32,
    )
    local_sums = jnp.einsum("st,tkp->skp", member, tile_terms, precision=lax.Precision.HIGHEST)
    received = lax.all_to_all(local_sums, "mk", split_axis=1, concat_axis=0, tiled=True)
    firsts = tile_chrom.reshape(mk_count, tile_dev)[:, 0]
    sources = (firsts[:, None] + jnp.arange(SPAN, dtype=jnp.int32)[None, :]).reshape(-1)
    assign = (jnp.arange(CHROMS, dtype=jnp.int32)[:, None] == sources[None, :]).astype(jnp.float32)
    chrom_sums = jnp.einsum("cj,jkp->ckp", assign, received, precision=lax.Precision.HIGHEST)
    combined = jnp.sum(chrom_sums, axis=0)
    loco_out = (phen_share[None] - combined[None] + chrom_sums).astype(jnp.bfloat16)
    return (updated, loco_out)


VMEM = pltpu.MemorySpace.VMEM
NT = (((1,), (1,)), ((), ()))


class Steps:
    def __init__(self, genotypes):
        self.genotypes = genotypes
        self.token = jnp.zeros((8, 128), jnp.float32)

    def call(self, body, outs, scalars=(), args=(), streamed=False, scratch=(), after=(), into=None):
        geno = self.genotypes
        tiles = geno.shape[1] // TILE
        after = list(after) + [into] * (into is not None)
        skip = 1 + len(after)
        filled = [] if into is None else [jax.ShapeDtypeStruct(into.shape, into.dtype)]
        count = skip + len(scalars) + len(args)

        def kernel(*refs):
            ins, rest = list(refs[skip:count]), list(refs[count:])
            if streamed:
                source = rest.pop(0)
                held, arrived = rest[1 + len(outs) : 3 + len(outs)]
                del rest[1 + len(outs) : 3 + len(outs)]
                copies = []
                for part in range(LOADS):
                    columns = pl.ds(part * geno.shape[1] // LOADS, geno.shape[1] // LOADS)
                    copies.append(pltpu.make_async_copy(source.at[:, columns], held.at[:, columns], arrived.at[part]))
                for copy in copies:
                    copy.start()

                def need(tile):
                    if tile * LOADS % tiles == 0:
                        copies[tile * LOADS // tiles].wait()

                ins += [held, need]
            body(*ins, *rest[1:])

        anywhere = pl.BlockSpec(memory_space=pl.ANY)
        stream_scratch = [pltpu.VMEM(geno.shape, geno.dtype), pltpu.SemaphoreType.DMA((LOADS,))] if streamed else []
        token, *results = pl.pallas_call(
            kernel,
            out_shape=[jax.ShapeDtypeStruct(self.token.shape, self.token.dtype), *outs, *filled],
            in_specs=[anywhere] * skip
            + [pl.BlockSpec(memory_space=pltpu.SMEM)] * len(scalars)
            + [pl.BlockSpec(memory_space=VMEM)] * len(args)
            + [anywhere] * streamed,
            out_specs=[anywhere] + [pl.BlockSpec(memory_space=VMEM)] * len(outs) + [anywhere] * len(filled),
            scratch_shapes=stream_scratch + list(scratch),
            input_output_aliases={0: 0} if into is None else {0: 0, skip - 1: 1 + len(outs)},
            cost_estimate=pl.CostEstimate(flops=1, bytes_accessed=1, transcendentals=0),
            compiler_params=pltpu.CompilerParams(vmem_limit_bytes=12 * 2**20),
        )(self.token, *after, *scalars, *[pltpu.with_memory_space_constraint(a, VMEM) for a in args], *[pltpu.with_memory_space_constraint(geno, pltpu.MemorySpace.HBM)] * streamed)
        if CHAIN:
            self.token = token
        return results


def columns_of(tile):
    return slice(tile * TILE, (tile + 1) * TILE)


def place():
    return lax.axis_index("pp") * 2 + lax.axis_index("sub"), lax.axis_index("mk")


def row_at(start, height):
    return pl.ds(pl.multiple_of(start, 16), height)


def piece_of(refs, tile):
    each = refs[0].shape[1] // TILE
    return refs[tile // each], columns_of(tile % each)


def predict_body(own, across, beside, corner, geno, need, keep, send, product):
    odd = place()[1] % 2
    half = 2 * own.shape[0]
    for tile in range(geno.shape[1] // TILE):
        part = columns_of(tile)
        rows = jnp.concatenate([own[:, part], across[:, part], beside[:, part], corner[:, part]], axis=0)
        need(tile)
        term = lax.dot_general(rows, geno[:, part], NT, preferred_element_type=jnp.float32)
        product[...] = term if tile == 0 else product[...] + term
    keep[...] = product[row_at(odd * half, half), :]
    send[...] = product[row_at(half - odd * half, half), :].astype(send.dtype)


def two_body(keep, came, two):
    two[...] = (keep[...] + came[...].astype(jnp.float32)).astype(two.dtype)


def residual_body(shard, low, phen, two, came, residual):
    me, depth = place()
    height = two.shape[0] // 2
    for block in range(2):
        at = slice(block * height, (block + 1) * height)
        prediction = two[at, :].astype(jnp.float32) + came[at, :].astype(jnp.float32)
        start = (me ^ (depth % 2) ^ (2 * block)) * shard + low
        measured = phen[row_at(start, height), :].astype(jnp.float32)
        residual[at, :] = (measured - prediction).astype(residual.dtype)


def score_body(low, mine, other, geno, need, keep, *sends):
    even = place()[1] % 2 == 0
    half = keep.shape[0]
    height, block = half // 2, mine.shape[0] // 2

    def rows_of(ref):
        return jnp.concatenate([ref[low : low + height], ref[block + low : block + low + height]], axis=0)

    first = jnp.where(even, rows_of(mine), rows_of(other))
    second = jnp.where(even, rows_of(other), rows_of(mine))
    rows = jnp.concatenate([first, second], axis=0)
    for tile in range(geno.shape[1] // TILE):
        part = columns_of(tile)
        need(tile)
        product = jnp.dot(rows, geno[:, part], preferred_element_type=jnp.float32)
        keep[:, part] = product[:half]
        send, inner = piece_of(sends, tile)
        send[:, inner] = product[half:].astype(send.dtype)


def chip_body(keep, *refs):
    *came, chip, send = refs
    height = keep.shape[0] // 2
    for tile in range(keep.shape[1] // TILE):
        part = columns_of(tile)
        ref, inner = piece_of(came, tile)
        total = keep[:, part] + ref[:, inner].astype(jnp.float32)
        chip[:, part] = total
        send[:height, part] = total[height:].astype(send.dtype)
        send[height:, part] = total[:height].astype(send.dtype)


def denoise_body(marker_root, people_root, low, first, own, across, chip, came, coefs, coefs_across, *refs):
    *updated, whole, stored = refs
    height = updated[0].shape[0] // 2
    at = slice(low, low + height)
    coef = jnp.concatenate([coefs[first : first + height], coefs_across[first : first + height]], axis=0)
    base, curve, gain = coef[:, 0:1], coef[:, 1:2], coef[:, 2:3]
    for tile in range(own.shape[1] // TILE):
        part = columns_of(tile)
        scores = chip[:, part] + came[:, part].astype(jnp.float32)
        estimate = jnp.concatenate([own[at, part], across[at, part]], axis=0).astype(jnp.float32)
        observed = marker_root * estimate + scores * (1.0 / people_root)
        log_odds = base + curve * observed * observed
        posterior = jax.nn.sigmoid(log_odds) * gain * observed
        ref, inner = piece_of(updated, tile)
        ref[:, inner] = (posterior * (1.0 / marker_root)).astype(ref.dtype)
    copies, width = [], updated[0].shape[1]
    for at, ref in enumerate(updated):
        target = whole.at[pl.ds(first, height), pl.ds(at * width, width)]
        copies.append(pltpu.make_async_copy(ref.at[pl.ds(0, height)], target, stored.at[at]))
    for copy in copies:
        copy.start()
    for copy in copies:
        copy.wait()


def chrom_body(labels, *refs):
    own, beside, (geno, need, *outs, acc) = refs[:SPLIT], refs[SPLIT : 2 * SPLIT], refs[2 * SPLIT :]
    me, depth = place()
    height = own[0].shape[0] // 2
    base = depth * (geno.shape[1] // TILE)
    starts = []
    for to in range(len(outs)):
        bits = me ^ depth ^ to
        starts.append(((bits % 2) * 2 + bits // 2) * height)
    for out in outs:
        out[...] = jnp.zeros_like(out)
    for tile in range(geno.shape[1] // TILE):
        part = columns_of(tile)
        halves = [ref[:, inner] for ref, inner in (piece_of(own, tile), piece_of(beside, tile))]
        rows = jnp.concatenate(halves, axis=0)
        need(tile)
        product = lax.dot_general(rows, geno[:, part], NT, preferred_element_type=jnp.float32)
        if tile == 0:
            acc[...] = product
        else:
            same = (labels[base + tile] == labels[base + tile - 1]).astype(jnp.float32)
            acc[...] = acc[...] * same + product
        slot = labels[base + tile] - labels[base]
        for start, out in zip(starts, outs):
            out[slot] = acc[row_at(start, height), :].astype(out.dtype)


def loco_body(row, shard, tiles, labels, phen, *refs):
    *sums, out, base, acc, stage, done = refs
    height = base.shape[0]
    _, depth = place()
    firsts = [labels[(depth ^ step) * tiles] for step in range(len(sums))]
    total = jnp.zeros(base.shape, jnp.float32)
    for part in sums:
        for slot in range(SPAN):
            total = total + part[slot].astype(jnp.float32)
    base[...] = phen[row_at(depth * shard + row, height), :].astype(jnp.float32) - total

    def copy(chrom):
        return pltpu.make_async_copy(stage.at[chrom], out.at[chrom, pl.ds(row, height)], done.at[chrom])

    def step(chrom, carry):
        acc[...] = base[...]
        for first, part in zip(firsts, sums):
            slot = chrom - first

            @pl.when((slot >= 0) & (slot < SPAN))
            def _():
                acc[...] += part[slot].astype(jnp.float32)

        stage[chrom] = acc[...].astype(stage.dtype)
        copy(chrom).start()
        return carry

    lax.fori_loop(0, CHROMS, step, 0)

    def finish(chrom, carry):
        copy(chrom).wait()
        return carry

    lax.fori_loop(0, CHROMS, finish, 0)


def leave_out(loco, token, shape, row, height, tiles, labels, phen, sums):
    people = phen.shape[1]
    anywhere = pl.BlockSpec(memory_space=pl.ANY)
    specs = [anywhere, pl.BlockSpec(memory_space=pltpu.SMEM)] + [pl.BlockSpec(memory_space=VMEM)] * (1 + len(sums))
    args = [token, labels] + [pltpu.with_memory_space_constraint(a, VMEM) for a in (phen, *sums)]
    before, aliases = 1, {0: 1}
    if loco is not None:
        specs, args, before, aliases = [anywhere] + specs, [loco] + args, 2, {0: 0, 1: 1}

    def body(*refs):
        ins, (out, _, *scratch) = refs[before : len(args)], refs[len(args) :]
        loco_body(row, shape[1], tiles, *ins, out, *scratch)

    return pl.pallas_call(
        body,
        out_shape=[jax.ShapeDtypeStruct(shape, jnp.bfloat16), jax.ShapeDtypeStruct(token.shape, token.dtype)],
        in_specs=specs,
        out_specs=[anywhere, anywhere],
        scratch_shapes=[pltpu.VMEM((height, people), jnp.float32)] * 2
        + [pltpu.VMEM((shape[0], height, people), jnp.bfloat16), pltpu.SemaphoreType.DMA((shape[0],))],
        input_output_aliases=aliases,
        cost_estimate=pl.CostEstimate(flops=1, bytes_accessed=1, transcendentals=0),
        compiler_params=pltpu.CompilerParams(vmem_limit_bytes=8 * 2**20),
    )(*args)


def piece_steps(genotypes, estimate, phenotypes, prior_logit, slab_var, noise_var, tile_chrom):
    people_dev, mark_dev = genotypes.shape
    shard = estimate.shape[0]
    mk_count = lax.axis_size("mk")
    people_count = lax.axis_size(("pp", "sub"))
    marker_root = math.sqrt(mark_dev * mk_count)
    people_root = math.sqrt(people_dev * people_count)
    tile_dev = mark_dev // TILE
    swap = [(0, 1), (1, 0)]

    def along(step):
        return [(i, i ^ step) for i in range(mk_count)]

    firsts, row = [], 0
    for part in FIRST:
        firsts.append((row, shard * part // sum(FIRST)))
        row += firsts[-1][1]
    seconds = [(of, firsts[of][1] * a // n, firsts[of][1] * b // n - firsts[of][1] * a // n) for of, a, b, n in SECOND]

    own = [estimate[row : row + height] for row, height in firsts]
    across = [lax.ppermute(one, "pp", swap) for one in own]
    beside = [lax.ppermute(one, "sub", swap) for one in own]
    corner = [lax.ppermute(one, "sub", swap) for one in across]
    spread = slab_var + noise_var
    coefs = jnp.stack(
        [prior_logit + 0.5 * jnp.log(noise_var / spread), 0.5 * (1.0 / noise_var - 1.0 / spread), slab_var / spread],
        axis=1,
    )
    coefs_across = lax.ppermute(coefs, "pp", swap)
    steps, whole, loco = Steps(genotypes), jnp.zeros(estimate.shape, estimate.dtype), None
    before, after = [{} for _ in firsts], [{} for _ in seconds]
    f32, bf16 = jnp.float32, jnp.bfloat16
    for stage, at in ORDER:
        if stage in ("pred", "two", "res"):
            now, (row, height) = before[at], firsts[at]
        else:
            now, (of, low, height) = after[at], seconds[at]
            row = firsts[of][0] + low
        half, wide = (2 * height, people_dev), (2 * height, mark_dev)
        narrow = pltpu.VMEM((2 * height, mark_dev // SPLIT), bf16)
        if stage == "pred":
            keep, send = steps.call(
                predict_body,
                [pltpu.VMEM(half, f32), pltpu.VMEM(half, bf16)],
                args=[own[at], across[at], beside[at], corner[at]],
                streamed=True,
                scratch=[pltpu.VMEM((4 * height, people_dev), f32)],
            )
            now["pred"] = keep, lax.ppermute(send, "mk", along(1))
        elif stage == "two":
            (two,) = steps.call(two_body, [pltpu.VMEM(half, bf16)], args=now["pred"])
            now["two"] = two, lax.ppermute(two, "mk", along(2))
        elif stage == "res":
            body = functools.partial(residual_body, shard, row)
            (residual,) = steps.call(body, [pltpu.VMEM(half, bf16)], args=[phenotypes, *now["two"]])
            now["res"] = residual, lax.ppermute(residual, "mk", along(1))
        elif stage == "score":
            keep, *sends = steps.call(
                functools.partial(score_body, low),
                [pltpu.VMEM(wide, f32)] + [narrow] * SPLIT,
                args=before[of]["res"],
                streamed=True,
                after=[coefs_across],
            )
            now["score"] = [keep] + [lax.ppermute(send, "sub", swap) for send in sends]
        elif stage == "chip":
            chip, send = steps.call(chip_body, [pltpu.VMEM(wide, f32), pltpu.VMEM(wide, bf16)], args=now["score"])
            now["chip"] = chip, lax.ppermute(send, "pp", swap)
        elif stage == "den":
            *updated, whole = steps.call(
                functools.partial(denoise_body, marker_root, people_root, low, row),
                [narrow] * SPLIT,
                args=[own[of], across[of], *now["chip"], coefs, coefs_across],
                scratch=[pltpu.SemaphoreType.DMA((SPLIT,))],
                into=whole,
            )
            now["den"] = updated + [lax.ppermute(one, "sub", swap) for one in updated]
        elif stage == "chrom":
            sums = steps.call(
                chrom_body,
                [pltpu.VMEM((SPAN, height, people_dev), bf16)] * mk_count,
                [tile_chrom],
                now["den"],
                streamed=True,
                scratch=[pltpu.VMEM((4 * height, people_dev), f32)],
            )
            now["chrom"] = [sums[0]] + [lax.ppermute(sums[step], "mk", along(step)) for step in range(1, mk_count)]
        else:
            shape = (CHROMS, shard, people_dev)
            loco, token = leave_out(
                loco, steps.token, shape, row, height, tile_dev, tile_chrom, phenotypes, now["chrom"]
            )
            if CHAIN:
                steps.token = token
    return (whole, loco)


def solution(mesh):
    placed = (
        P(("grp", "pp", "sub"), "mk"),
        P(("grp", "pp", "sub"), "mk"),
        P("grp", ("pp", "sub")),
        P(("grp", "pp", "sub")),
        P(("grp", "pp", "sub")),
        P(("grp", "pp", "sub")),
        P("grp"),
    )
    by_pieces = (mesh.shape["pp"], mesh.shape["sub"], mesh.shape["mk"]) == (2, 2, 4)
    return jax.shard_map(
        piece_steps if by_pieces else whole_mesh_steps,
        mesh=mesh,
        in_specs=placed,
        out_specs=(P(("grp", "pp", "sub"), "mk"), P("grp", "mk", ("pp", "sub"))),
        check_vma=False,
    )
```

```python
import functools
import math

import jax
import jax.numpy as jnp
from jax import lax
from jax.experimental import pallas as pl
from jax.experimental.pallas import tpu as pltpu
from jax.sharding import PartitionSpec as P

CHROMS = 22
TILE = 512
SPAN = 6
LOADS = 2
SPLIT = 4
SCORE_SPLIT = 8
TOGETHER = ()
CHAIN = True
RESIDENT = True
FIRST = (1, 1)
SECOND = ((0, 0, 1, 1), (1, 0, 1, 1))
ORDER = (('pred', 0), ('two', 0), ('pred', 1), ('res', 0), ('two', 1), ('score', 0), ('res', 1), ('chip', 0), ('score', 1), ('chip', 1), ('den', 0), ('chrom', 0), ('den', 1), ('chrom', 1), ('leave', 0), ('leave', 1))


def denoise(estimate, scores, prior_logit, slab_var, noise_var, marker_root, people_root):
    observed = marker_root * estimate.astype(jnp.float32) + scores * (1.0 / people_root)
    slab_col = slab_var[:, None]
    noise_col = noise_var[:, None]
    spread = slab_col + noise_col
    log_odds = (
        prior_logit[:, None]
        + 0.5 * jnp.log(noise_col / spread)
        + 0.5 * observed * observed * (1.0 / noise_col - 1.0 / spread)
    )
    posterior = jax.nn.sigmoid(log_odds) * (slab_col / spread) * observed
    return (posterior * (1.0 / marker_root)).astype(jnp.bfloat16)


def whole_mesh_steps(genotypes, estimate, phenotypes, prior_logit, slab_var, noise_var, tile_chrom):
    people_dev, mark_dev = genotypes.shape
    mk_count = lax.axis_size("mk")
    people_count = lax.axis_size(("pp", "sub"))
    traits = phenotypes.shape[0]
    partial_pred = lax.dot_general(
        lax.all_gather(estimate, ("pp", "sub"), axis=0, tiled=True),
        genotypes,
        (((1,), (1,)), ((), ())),
        preferred_element_type=jnp.float32,
    )
    share_rows = traits // mk_count
    offset = lax.axis_index("mk") * share_rows
    phen_share = lax.dynamic_slice_in_dim(phenotypes, offset, share_rows, 0).astype(jnp.float32)
    prediction = lax.psum(partial_pred, "mk")
    residual = (phenotypes.astype(jnp.float32) - prediction).astype(jnp.bfloat16)
    scores = lax.psum_scatter(
        jnp.dot(residual, genotypes, preferred_element_type=jnp.float32),
        ("pp", "sub"),
        scatter_dimension=0,
        tiled=True,
    )
    updated = denoise(
        estimate,
        scores,
        prior_logit,
        slab_var,
        noise_var,
        math.sqrt(mark_dev * mk_count),
        math.sqrt(people_dev * people_count),
    )
    tile_dev = mark_dev // TILE
    own_tiles = lax.dynamic_slice_in_dim(tile_chrom, lax.axis_index("mk") * tile_dev, tile_dev, 0)
    labels = own_tiles[0] + jnp.arange(SPAN, dtype=jnp.int32)
    member = (labels[:, None] == own_tiles[None, :]).astype(jnp.float32)
    geno_tiles = genotypes.reshape(people_dev, tile_dev, TILE)
    shard_rows = lax.all_gather(updated, ("pp", "sub"), axis=0, tiled=True)
    tile_terms = jnp.einsum(
        "kta,pta->tkp",
        shard_rows.reshape(shard_rows.shape[0], tile_dev, TILE),
        geno_tiles,
        preferred_element_type=jnp.float32,
    )
    local_sums = jnp.einsum("st,tkp->skp", member, tile_terms, precision=lax.Precision.HIGHEST)
    received = lax.all_to_all(local_sums, "mk", split_axis=1, concat_axis=0, tiled=True)
    firsts = tile_chrom.reshape(mk_count, tile_dev)[:, 0]
    sources = (firsts[:, None] + jnp.arange(SPAN, dtype=jnp.int32)[None, :]).reshape(-1)
    assign = (jnp.arange(CHROMS, dtype=jnp.int32)[:, None] == sources[None, :]).astype(jnp.float32)
    chrom_sums = jnp.einsum("cj,jkp->ckp", assign, received, precision=lax.Precision.HIGHEST)
    combined = jnp.sum(chrom_sums, axis=0)
    loco_out = (phen_share[None] - combined[None] + chrom_sums).astype(jnp.bfloat16)
    return (updated, loco_out)


VMEM = pltpu.MemorySpace.VMEM
NT = (((1,), (1,)), ((), ()))


class Steps:
    def __init__(self, genotypes):
        self.genotypes = genotypes
        self.token = jnp.zeros((8, 128), jnp.float32)

    def call(self, body, outs, scalars=(), args=(), streamed=False, scratch=(), after=(), into=None, fresh=None):
        geno = self.genotypes
        tiles = geno.shape[1] // TILE
        after = list(after) + [into] * (into is not None)
        skip = 1 + len(after)
        filled = [fresh] * (fresh is not None) + [jax.ShapeDtypeStruct(one.shape, one.dtype) for one in [into] * (into is not None)]
        count = skip + len(scalars) + len(args)

        def kernel(*refs):
            ins, rest = list(refs[skip:count]), list(refs[count:])
            if streamed and RESIDENT:
                ins += [rest.pop(0), lambda tile: None]
            elif streamed:
                source = rest.pop(0)
                held, arrived = rest[1 + len(outs) : 3 + len(outs)]
                del rest[1 + len(outs) : 3 + len(outs)]
                copies = []
                for part in range(LOADS):
                    columns = pl.ds(part * geno.shape[1] // LOADS, geno.shape[1] // LOADS)
                    copies.append(pltpu.make_async_copy(source.at[:, columns], held.at[:, columns], arrived.at[part]))
                for copy in copies:
                    copy.start()

                def need(tile):
                    if tile * LOADS % tiles == 0:
                        copies[tile * LOADS // tiles].wait()

                ins += [held, need]
            body(*ins, *rest[1:])

        anywhere = pl.BlockSpec(memory_space=pl.ANY)
        stream_scratch = [pltpu.VMEM(geno.shape, geno.dtype), pltpu.SemaphoreType.DMA((LOADS,))] if streamed and not RESIDENT else []
        token, *results = pl.pallas_call(
            kernel,
            out_shape=[jax.ShapeDtypeStruct(self.token.shape, self.token.dtype), *outs, *filled],
            in_specs=[anywhere] * skip
            + [pl.BlockSpec(memory_space=pltpu.SMEM)] * len(scalars)
            + [pl.BlockSpec(memory_space=VMEM)] * len(args)
            + [pl.BlockSpec(memory_space=VMEM) if RESIDENT else anywhere] * streamed,
            out_specs=[anywhere] + [pl.BlockSpec(memory_space=VMEM)] * len(outs) + [anywhere] * len(filled),
            scratch_shapes=stream_scratch + list(scratch),
            input_output_aliases={0: 0} if into is None else {0: 0, skip - 1: 1 + len(outs)},
            cost_estimate=pl.CostEstimate(flops=1, bytes_accessed=1, transcendentals=0),
            compiler_params=pltpu.CompilerParams(vmem_limit_bytes=12 * 2**20),
        )(self.token, *after, *scalars, *[pltpu.with_memory_space_constraint(a, VMEM) for a in args], *[pltpu.with_memory_space_constraint(geno, VMEM if RESIDENT else pltpu.MemorySpace.HBM)] * streamed)
        if CHAIN:
            self.token = token
        return results


def columns_of(tile):
    return slice(tile * TILE, (tile + 1) * TILE)


def place():
    return lax.axis_index("pp") * 2 + lax.axis_index("sub"), lax.axis_index("mk")


def row_at(start, height):
    return pl.ds(pl.multiple_of(start, 16), height)


def piece_of(refs, tile):
    each = refs[0].shape[1] // TILE
    return refs[tile // each], columns_of(tile % each)


def predict_body(own, across, beside, corner, geno, need, keep, send, product):
    odd = place()[1] % 2
    half = 2 * own.shape[0]
    for tile in range(geno.shape[1] // TILE):
        part = columns_of(tile)
        rows = jnp.concatenate([own[:, part], across[:, part], beside[:, part], corner[:, part]], axis=0)
        need(tile)
        term = lax.dot_general(rows, geno[:, part], NT, preferred_element_type=jnp.float32)
        product[...] = term if tile == 0 else product[...] + term
    keep[...] = product[row_at(odd * half, half), :]
    send[...] = product[row_at(half - odd * half, half), :].astype(send.dtype)


def two_body(keep, came, two):
    two[...] = (keep[...] + came[...].astype(jnp.float32)).astype(two.dtype)


def residual_body(shard, low, phen, two, came, residual):
    me, depth = place()
    height = two.shape[0] // 2
    for block in range(2):
        at = slice(block * height, (block + 1) * height)
        prediction = two[at, :].astype(jnp.float32) + came[at, :].astype(jnp.float32)
        start = (me ^ (depth % 2) ^ (2 * block)) * shard + low
        measured = phen[row_at(start, height), :].astype(jnp.float32)
        residual[at, :] = (measured - prediction).astype(residual.dtype)


def score_body(low, mine, other, geno, need, keep, *sends):
    even = place()[1] % 2 == 0
    half = keep.shape[0]
    height, block = half // 2, mine.shape[0] // 2

    def rows_of(ref):
        return jnp.concatenate([ref[low : low + height], ref[block + low : block + low + height]], axis=0)

    first = jnp.where(even, rows_of(mine), rows_of(other))
    second = jnp.where(even, rows_of(other), rows_of(mine))
    rows = jnp.concatenate([first, second], axis=0)
    for tile in range(geno.shape[1] // TILE):
        part = columns_of(tile)
        need(tile)
        product = jnp.dot(rows, geno[:, part], preferred_element_type=jnp.float32)
        keep[:, part] = product[:half]
        send, inner = piece_of(sends, tile)
        send[:, inner] = product[half:].astype(send.dtype)


def chip_body(keep, *refs):
    *came, chip, send = refs
    height = keep.shape[0] // 2
    for tile in range(keep.shape[1] // TILE):
        part = columns_of(tile)
        ref, inner = piece_of(came, tile)
        total = keep[:, part] + ref[:, inner].astype(jnp.float32)
        chip[:, part] = total
        send[:height, part] = total[height:].astype(send.dtype)
        send[height:, part] = total[:height].astype(send.dtype)


def denoise_body(marker_root, people_root, low, first, own, across, chip, came, coefs, coefs_across, *refs):
    *updated, whole, stored = refs
    height = updated[0].shape[0] // 2
    at = slice(low, low + height)
    coef = jnp.concatenate([coefs[first : first + height], coefs_across[first : first + height]], axis=0)
    base, curve, gain = coef[:, 0:1], coef[:, 1:2], coef[:, 2:3]
    for tile in range(own.shape[1] // TILE):
        part = columns_of(tile)
        scores = chip[:, part] + came[:, part].astype(jnp.float32)
        estimate = jnp.concatenate([own[at, part], across[at, part]], axis=0).astype(jnp.float32)
        observed = marker_root * estimate + scores * (1.0 / people_root)
        log_odds = base + curve * observed * observed
        posterior = jax.nn.sigmoid(log_odds) * gain * observed
        ref, inner = piece_of(updated, tile)
        ref[:, inner] = (posterior * (1.0 / marker_root)).astype(ref.dtype)
    copies, width = [], updated[0].shape[1]
    for at, ref in enumerate(updated):
        target = whole.at[pl.ds(first, height), pl.ds(at * width, width)]
        copies.append(pltpu.make_async_copy(ref.at[pl.ds(0, height)], target, stored.at[at]))
    for copy in copies:
        copy.start()
    for copy in copies:
        copy.wait()


def chrom_body(together, labels, *refs):
    own, beside, (geno, need, *outs, acc) = refs[:SPLIT], refs[SPLIT : 2 * SPLIT], refs[2 * SPLIT :]
    if together:
        outs = [outs[0].at[to] for to in range(outs[0].shape[0])]
    me, depth = place()
    height = own[0].shape[0] // 2
    base = depth * (geno.shape[1] // TILE)
    starts = []
    for to in range(len(outs)):
        bits = me ^ to if together else me ^ depth ^ to
        starts.append(((bits % 2) * 2 + bits // 2) * height)
    for out in outs:
        out[...] = jnp.zeros(out.shape, out.dtype)
    for tile in range(geno.shape[1] // TILE):
        part = columns_of(tile)
        halves = [ref[:, inner] for ref, inner in (piece_of(own, tile), piece_of(beside, tile))]
        rows = jnp.concatenate(halves, axis=0)
        need(tile)
        product = lax.dot_general(rows, geno[:, part], NT, preferred_element_type=jnp.float32)
        if tile == 0:
            acc[...] = product
        else:
            same = (labels[base + tile] == labels[base + tile - 1]).astype(jnp.float32)
            acc[...] = acc[...] * same + product
        slot = labels[base + tile] - labels[base]
        for start, out in zip(starts, outs):
            out[slot] = acc[row_at(start, height), :].astype(out.dtype)


def loco_body(row, shard, tiles, count, labels, phen, *refs):
    *sums, out, base, acc, stage, done = refs
    height = base.shape[0]
    _, depth = place()
    if len(sums) == 1:
        firsts, sums = [labels[step * tiles] for step in range(count)], [sums[0].at[step] for step in range(count)]
    else:
        firsts = [labels[(depth ^ step) * tiles] for step in range(count)]
    total = jnp.zeros(base.shape, jnp.float32)
    for part in sums:
        for slot in range(SPAN):
            total = total + part[slot].astype(jnp.float32)
    base[...] = phen[row_at(depth * shard + row, height), :].astype(jnp.float32) - total

    def copy(chrom):
        return pltpu.make_async_copy(stage.at[chrom], out.at[chrom, pl.ds(row, height)], done.at[chrom])

    def step(chrom, carry):
        acc[...] = base[...]
        for first, part in zip(firsts, sums):
            slot = chrom - first

            @pl.when((slot >= 0) & (slot < SPAN))
            def _():
                acc[...] += part[slot].astype(jnp.float32)

        stage[chrom] = acc[...].astype(stage.dtype)
        copy(chrom).start()
        return carry

    lax.fori_loop(0, CHROMS, step, 0)

    def finish(chrom, carry):
        copy(chrom).wait()
        return carry

    lax.fori_loop(0, CHROMS, finish, 0)


def leave_out(loco, token, shape, row, height, tiles, count, labels, phen, sums):
    people = phen.shape[1]
    anywhere = pl.BlockSpec(memory_space=pl.ANY)
    specs = [anywhere, pl.BlockSpec(memory_space=pltpu.SMEM)] + [pl.BlockSpec(memory_space=VMEM)] * (1 + len(sums))
    args = [token, labels] + [pltpu.with_memory_space_constraint(a, VMEM) for a in (phen, *sums)]
    before, aliases = 1, {0: 1}
    if loco is not None:
        specs, args, before, aliases = [anywhere] + specs, [loco] + args, 2, {0: 0, 1: 1}

    def body(*refs):
        ins, (out, _, *scratch) = refs[before : len(args)], refs[len(args) :]
        loco_body(row, shape[1], tiles, count, *ins, out, *scratch)

    return pl.pallas_call(
        body,
        out_shape=[jax.ShapeDtypeStruct(shape, jnp.bfloat16), jax.ShapeDtypeStruct(token.shape, token.dtype)],
        in_specs=specs,
        out_specs=[anywhere, anywhere],
        scratch_shapes=[pltpu.VMEM((height, people), jnp.float32)] * 2
        + [pltpu.VMEM((shape[0], height, people), jnp.bfloat16), pltpu.SemaphoreType.DMA((shape[0],))],
        input_output_aliases=aliases,
        cost_estimate=pl.CostEstimate(flops=1, bytes_accessed=1, transcendentals=0),
        compiler_params=pltpu.CompilerParams(vmem_limit_bytes=8 * 2**20),
    )(*args)


def piece_steps(genotypes, estimate, phenotypes, prior_logit, slab_var, noise_var, tile_chrom):
    people_dev, mark_dev = genotypes.shape
    shard = estimate.shape[0]
    mk_count = lax.axis_size("mk")
    people_count = lax.axis_size(("pp", "sub"))
    marker_root = math.sqrt(mark_dev * mk_count)
    people_root = math.sqrt(people_dev * people_count)
    tile_dev = mark_dev // TILE
    swap = [(0, 1), (1, 0)]

    def along(step):
        return [(i, i ^ step) for i in range(mk_count)]

    firsts, row = [], 0
    for part in FIRST:
        firsts.append((row, shard * part // sum(FIRST)))
        row += firsts[-1][1]
    seconds = [(of, firsts[of][1] * a // n, firsts[of][1] * b // n - firsts[of][1] * a // n) for of, a, b, n in SECOND]

    own = [estimate[row : row + height] for row, height in firsts]
    across = [lax.ppermute(one, "pp", swap) for one in own]
    beside = [lax.ppermute(one, "sub", swap) for one in own]
    corner = [lax.ppermute(one, "sub", swap) for one in across]
    spread = slab_var + noise_var
    coefs = jnp.stack(
        [prior_logit + 0.5 * jnp.log(noise_var / spread), 0.5 * (1.0 / noise_var - 1.0 / spread), slab_var / spread],
        axis=1,
    )
    coefs_across = lax.ppermute(coefs, "pp", swap)
    steps, whole, loco = Steps(genotypes), None, None
    before, after = [{} for _ in firsts], [{} for _ in seconds]
    f32, bf16 = jnp.float32, jnp.bfloat16
    for stage, at in ORDER:
        if stage in ("pred", "two", "res"):
            now, (row, height) = before[at], firsts[at]
        else:
            now, (of, low, height) = after[at], seconds[at]
            row = firsts[of][0] + low
        half, wide = (2 * height, people_dev), (2 * height, mark_dev)
        narrow = pltpu.VMEM((2 * height, mark_dev // SPLIT), bf16)
        if stage == "pred":
            keep, send = steps.call(
                predict_body,
                [pltpu.VMEM(half, f32), pltpu.VMEM(half, bf16)],
                args=[own[at], across[at], beside[at], corner[at]],
                streamed=True,
                scratch=[pltpu.VMEM((4 * height, people_dev), f32)],
            )
            now["pred"] = keep, lax.ppermute(send, "mk", along(1))
        elif stage == "two":
            (two,) = steps.call(two_body, [pltpu.VMEM(half, bf16)], args=now["pred"])
            now["two"] = two, lax.ppermute(two, "mk", along(2))
        elif stage == "res":
            body = functools.partial(residual_body, shard, row)
            (residual,) = steps.call(body, [pltpu.VMEM(half, bf16)], args=[phenotypes, *now["two"]])
            now["res"] = residual, lax.ppermute(residual, "mk", along(1))
        elif stage == "score":
            keep, *sends = steps.call(
                functools.partial(score_body, low),
                [pltpu.VMEM(wide, f32)] + [pltpu.VMEM((2 * height, mark_dev // SCORE_SPLIT), bf16)] * SCORE_SPLIT,
                args=before[of]["res"],
                streamed=True,
                after=[coefs_across],
            )
            now["score"] = [keep] + [lax.ppermute(send, "sub", swap) for send in sends]
        elif stage == "chip":
            chip, send = steps.call(chip_body, [pltpu.VMEM(wide, f32), pltpu.VMEM(wide, bf16)], args=now["score"])
            now["chip"] = chip, lax.ppermute(send, "pp", swap)
        elif stage == "den":
            *updated, whole = steps.call(
                functools.partial(denoise_body, marker_root, people_root, low, row),
                [narrow] * SPLIT,
                args=[own[of], across[of], *now["chip"], coefs, coefs_across],
                scratch=[pltpu.SemaphoreType.DMA((SPLIT,))],
                into=whole,
                fresh=None if whole is not None else jax.ShapeDtypeStruct(estimate.shape, estimate.dtype),
            )
            now["den"] = updated + [lax.ppermute(one, "sub", swap) for one in updated]
        elif stage == "chrom":
            block, together = (SPAN, height, people_dev), at in TOGETHER
            sums = steps.call(
                functools.partial(chrom_body, together),
                [pltpu.VMEM((mk_count, *block), bf16)] if together else [pltpu.VMEM(block, bf16)] * mk_count,
                [tile_chrom],
                now["den"],
                streamed=True,
                scratch=[pltpu.VMEM((4 * height, people_dev), f32)],
            )
            if together:
                now["chrom"] = [lax.all_to_all(sums[0], "mk", 0, 0, tiled=True)]
            else:
                now["chrom"] = [sums[0]] + [lax.ppermute(sums[step], "mk", along(step)) for step in range(1, mk_count)]
        else:
            shape = (CHROMS, shard, people_dev)
            loco, token = leave_out(
                loco, steps.token, shape, row, height, tile_dev, mk_count, tile_chrom, phenotypes, now["chrom"]
            )
            if CHAIN:
                steps.token = token
    return (whole, loco)


def solution(mesh):
    placed = (
        P(("grp", "pp", "sub"), "mk"),
        P(("grp", "pp", "sub"), "mk"),
        P("grp", ("pp", "sub")),
        P(("grp", "pp", "sub")),
        P(("grp", "pp", "sub")),
        P(("grp", "pp", "sub")),
        P("grp"),
    )
    by_pieces = (mesh.shape["pp"], mesh.shape["sub"], mesh.shape["mk"]) == (2, 2, 4)
    return jax.shard_map(
        piece_steps if by_pieces else whole_mesh_steps,
        mesh=mesh,
        in_specs=placed,
        out_specs=(P(("grp", "pp", "sub"), "mk"), P("grp", "mk", ("pp", "sub"))),
        check_vma=False,
    )
```

```python
import functools
import math

import jax
import jax.numpy as jnp
from jax import lax
from jax.experimental import pallas as pl
from jax.experimental.pallas import tpu as pltpu
from jax.sharding import PartitionSpec as P

CHROMS = 22
TILE = 512
SPAN = 6
LOADS = 2
SPLIT = 4
SCORE_SPLIT = 8
TOGETHER = ()
CHAIN = True
RESIDENT = True
TOUCH = False
HOLD = True
FIRST = (1, 1)
SECOND = ((0, 0, 1, 1), (1, 0, 1, 1))
ORDER = (('pred', 0), ('two', 0), ('pred', 1), ('res', 0), ('two', 1), ('score', 0), ('res', 1), ('chip', 0), ('score', 1), ('chip', 1), ('den', 0), ('chrom', 0), ('den', 1), ('chrom', 1), ('leave', 0), ('leave', 1))


def denoise(estimate, scores, prior_logit, slab_var, noise_var, marker_root, people_root):
    observed = marker_root * estimate.astype(jnp.float32) + scores * (1.0 / people_root)
    slab_col = slab_var[:, None]
    noise_col = noise_var[:, None]
    spread = slab_col + noise_col
    log_odds = (
        prior_logit[:, None]
        + 0.5 * jnp.log(noise_col / spread)
        + 0.5 * observed * observed * (1.0 / noise_col - 1.0 / spread)
    )
    posterior = jax.nn.sigmoid(log_odds) * (slab_col / spread) * observed
    return (posterior * (1.0 / marker_root)).astype(jnp.bfloat16)


def whole_mesh_steps(genotypes, estimate, phenotypes, prior_logit, slab_var, noise_var, tile_chrom):
    people_dev, mark_dev = genotypes.shape
    mk_count = lax.axis_size("mk")
    people_count = lax.axis_size(("pp", "sub"))
    traits = phenotypes.shape[0]
    partial_pred = lax.dot_general(
        lax.all_gather(estimate, ("pp", "sub"), axis=0, tiled=True),
        genotypes,
        (((1,), (1,)), ((), ())),
        preferred_element_type=jnp.float32,
    )
    share_rows = traits // mk_count
    offset = lax.axis_index("mk") * share_rows
    phen_share = lax.dynamic_slice_in_dim(phenotypes, offset, share_rows, 0).astype(jnp.float32)
    prediction = lax.psum(partial_pred, "mk")
    residual = (phenotypes.astype(jnp.float32) - prediction).astype(jnp.bfloat16)
    scores = lax.psum_scatter(
        jnp.dot(residual, genotypes, preferred_element_type=jnp.float32),
        ("pp", "sub"),
        scatter_dimension=0,
        tiled=True,
    )
    updated = denoise(
        estimate,
        scores,
        prior_logit,
        slab_var,
        noise_var,
        math.sqrt(mark_dev * mk_count),
        math.sqrt(people_dev * people_count),
    )
    tile_dev = mark_dev // TILE
    own_tiles = lax.dynamic_slice_in_dim(tile_chrom, lax.axis_index("mk") * tile_dev, tile_dev, 0)
    labels = own_tiles[0] + jnp.arange(SPAN, dtype=jnp.int32)
    member = (labels[:, None] == own_tiles[None, :]).astype(jnp.float32)
    geno_tiles = genotypes.reshape(people_dev, tile_dev, TILE)
    shard_rows = lax.all_gather(updated, ("pp", "sub"), axis=0, tiled=True)
    tile_terms = jnp.einsum(
        "kta,pta->tkp",
        shard_rows.reshape(shard_rows.shape[0], tile_dev, TILE),
        geno_tiles,
        preferred_element_type=jnp.float32,
    )
    local_sums = jnp.einsum("st,tkp->skp", member, tile_terms, precision=lax.Precision.HIGHEST)
    received = lax.all_to_all(local_sums, "mk", split_axis=1, concat_axis=0, tiled=True)
    firsts = tile_chrom.reshape(mk_count, tile_dev)[:, 0]
    sources = (firsts[:, None] + jnp.arange(SPAN, dtype=jnp.int32)[None, :]).reshape(-1)
    assign = (jnp.arange(CHROMS, dtype=jnp.int32)[:, None] == sources[None, :]).astype(jnp.float32)
    chrom_sums = jnp.einsum("cj,jkp->ckp", assign, received, precision=lax.Precision.HIGHEST)
    combined = jnp.sum(chrom_sums, axis=0)
    loco_out = (phen_share[None] - combined[None] + chrom_sums).astype(jnp.bfloat16)
    return (updated, loco_out)


VMEM = pltpu.MemorySpace.VMEM
NT = (((1,), (1,)), ((), ()))


class Steps:
    def __init__(self, genotypes):
        self.genotypes = genotypes
        self.token = jnp.zeros((8, 128), jnp.float32)

    def call(self, body, outs, scalars=(), args=(), streamed=False, scratch=(), after=(), into=None, fresh=None):
        geno = self.genotypes
        tiles = geno.shape[1] // TILE
        given = streamed or TOUCH
        after = list(after) + [into] * (into is not None)
        skip = 1 + len(after)
        filled = [fresh] * (fresh is not None) + [jax.ShapeDtypeStruct(one.shape, one.dtype) for one in [into] * (into is not None)]
        count = skip + len(scalars) + len(args)

        def kernel(*refs):
            ins, rest = list(refs[skip:count]), list(refs[count:])
            if given and not streamed:
                rest.pop(0)
            if streamed and RESIDENT:
                ins += [rest.pop(0), lambda tile: None]
            elif streamed:
                source = rest.pop(0)
                held, arrived = rest[1 + len(outs) : 3 + len(outs)]
                del rest[1 + len(outs) : 3 + len(outs)]
                copies = []
                for part in range(LOADS):
                    columns = pl.ds(part * geno.shape[1] // LOADS, geno.shape[1] // LOADS)
                    copies.append(pltpu.make_async_copy(source.at[:, columns], held.at[:, columns], arrived.at[part]))
                for copy in copies:
                    copy.start()

                def need(tile):
                    if tile * LOADS % tiles == 0:
                        copies[tile * LOADS // tiles].wait()

                ins += [held, need]
            body(*ins, *rest[1:])

        anywhere = pl.BlockSpec(memory_space=pl.ANY)
        stream_scratch = [pltpu.VMEM(geno.shape, geno.dtype), pltpu.SemaphoreType.DMA((LOADS,))] if streamed and not RESIDENT else []
        token, *results = pl.pallas_call(
            kernel,
            out_shape=[jax.ShapeDtypeStruct(self.token.shape, self.token.dtype), *outs, *filled],
            in_specs=[anywhere] * skip
            + [pl.BlockSpec(memory_space=pltpu.SMEM)] * len(scalars)
            + [pl.BlockSpec(memory_space=VMEM)] * len(args)
            + [pl.BlockSpec(memory_space=VMEM) if RESIDENT else anywhere] * given,
            out_specs=[anywhere] + [pl.BlockSpec(memory_space=VMEM)] * len(outs) + [anywhere] * len(filled),
            scratch_shapes=stream_scratch + list(scratch),
            input_output_aliases={0: 0} if into is None else {0: 0, skip - 1: 1 + len(outs)},
            cost_estimate=pl.CostEstimate(flops=1, bytes_accessed=1, transcendentals=0),
            compiler_params=pltpu.CompilerParams(vmem_limit_bytes=12 * 2**20),
        )(self.token, *after, *scalars, *[pltpu.with_memory_space_constraint(a, VMEM) for a in args], *[pltpu.with_memory_space_constraint(geno, VMEM if RESIDENT else pltpu.MemorySpace.HBM)] * given)
        if CHAIN:
            self.token = token
        return results


def columns_of(tile):
    return slice(tile * TILE, (tile + 1) * TILE)


def place():
    return lax.axis_index("pp") * 2 + lax.axis_index("sub"), lax.axis_index("mk")


def row_at(start, height):
    return pl.ds(pl.multiple_of(start, 16), height)


def piece_of(refs, tile):
    each = refs[0].shape[1] // TILE
    return refs[tile // each], columns_of(tile % each)


def predict_body(own, across, beside, corner, geno, need, keep, send, product):
    odd = place()[1] % 2
    half = 2 * own.shape[0]
    for tile in range(geno.shape[1] // TILE):
        part = columns_of(tile)
        rows = jnp.concatenate([own[:, part], across[:, part], beside[:, part], corner[:, part]], axis=0)
        need(tile)
        term = lax.dot_general(rows, geno[:, part], NT, preferred_element_type=jnp.float32)
        product[...] = term if tile == 0 else product[...] + term
    keep[...] = product[row_at(odd * half, half), :]
    send[...] = product[row_at(half - odd * half, half), :].astype(send.dtype)


def two_body(keep, came, two):
    two[...] = (keep[...] + came[...].astype(jnp.float32)).astype(two.dtype)


def residual_body(shard, low, phen, two, came, residual):
    me, depth = place()
    height = two.shape[0] // 2
    for block in range(2):
        at = slice(block * height, (block + 1) * height)
        prediction = two[at, :].astype(jnp.float32) + came[at, :].astype(jnp.float32)
        start = (me ^ (depth % 2) ^ (2 * block)) * shard + low
        measured = phen[row_at(start, height), :].astype(jnp.float32)
        residual[at, :] = (measured - prediction).astype(residual.dtype)


def score_body(low, mine, other, geno, need, keep, *sends):
    even = place()[1] % 2 == 0
    half = keep.shape[0]
    height, block = half // 2, mine.shape[0] // 2

    def rows_of(ref):
        return jnp.concatenate([ref[low : low + height], ref[block + low : block + low + height]], axis=0)

    first = jnp.where(even, rows_of(mine), rows_of(other))
    second = jnp.where(even, rows_of(other), rows_of(mine))
    rows = jnp.concatenate([first, second], axis=0)
    for tile in range(geno.shape[1] // TILE):
        part = columns_of(tile)
        need(tile)
        product = jnp.dot(rows, geno[:, part], preferred_element_type=jnp.float32)
        keep[:, part] = product[:half]
        send, inner = piece_of(sends, tile)
        send[:, inner] = product[half:].astype(send.dtype)


def chip_body(keep, *refs):
    *came, chip, send = refs
    height = keep.shape[0] // 2
    for tile in range(keep.shape[1] // TILE):
        part = columns_of(tile)
        ref, inner = piece_of(came, tile)
        total = keep[:, part] + ref[:, inner].astype(jnp.float32)
        chip[:, part] = total
        send[:height, part] = total[height:].astype(send.dtype)
        send[height:, part] = total[:height].astype(send.dtype)


def denoise_body(marker_root, people_root, low, first, own, across, chip, came, coefs, coefs_across, *refs):
    *updated, whole, stored = refs
    height = updated[0].shape[0] // 2
    at = slice(low, low + height)
    coef = jnp.concatenate([coefs[first : first + height], coefs_across[first : first + height]], axis=0)
    base, curve, gain = coef[:, 0:1], coef[:, 1:2], coef[:, 2:3]
    for tile in range(own.shape[1] // TILE):
        part = columns_of(tile)
        scores = chip[:, part] + came[:, part].astype(jnp.float32)
        estimate = jnp.concatenate([own[at, part], across[at, part]], axis=0).astype(jnp.float32)
        observed = marker_root * estimate + scores * (1.0 / people_root)
        log_odds = base + curve * observed * observed
        posterior = jax.nn.sigmoid(log_odds) * gain * observed
        ref, inner = piece_of(updated, tile)
        ref[:, inner] = (posterior * (1.0 / marker_root)).astype(ref.dtype)
    copies, width = [], updated[0].shape[1]
    for at, ref in enumerate(updated):
        target = whole.at[pl.ds(first, height), pl.ds(at * width, width)]
        copies.append(pltpu.make_async_copy(ref.at[pl.ds(0, height)], target, stored.at[at]))
    for copy in copies:
        copy.start()
    for copy in copies:
        copy.wait()


def chrom_body(together, labels, *refs):
    own, beside, (geno, need, *outs, acc) = refs[:SPLIT], refs[SPLIT : 2 * SPLIT], refs[2 * SPLIT :]
    if together:
        outs = [outs[0].at[to] for to in range(outs[0].shape[0])]
    me, depth = place()
    height = own[0].shape[0] // 2
    base = depth * (geno.shape[1] // TILE)
    starts = []
    for to in range(len(outs)):
        bits = me ^ to if together else me ^ depth ^ to
        starts.append(((bits % 2) * 2 + bits // 2) * height)
    for out in outs:
        out[...] = jnp.zeros(out.shape, out.dtype)
    for tile in range(geno.shape[1] // TILE):
        part = columns_of(tile)
        halves = [ref[:, inner] for ref, inner in (piece_of(own, tile), piece_of(beside, tile))]
        rows = jnp.concatenate(halves, axis=0)
        need(tile)
        product = lax.dot_general(rows, geno[:, part], NT, preferred_element_type=jnp.float32)
        if tile == 0:
            acc[...] = product
        else:
            same = (labels[base + tile] == labels[base + tile - 1]).astype(jnp.float32)
            acc[...] = acc[...] * same + product
        slot = labels[base + tile] - labels[base]
        for start, out in zip(starts, outs):
            out[slot] = acc[row_at(start, height), :].astype(out.dtype)


def loco_body(row, shard, tiles, count, labels, phen, *refs):
    *sums, out, base, acc, stage, done = refs
    height = base.shape[0]
    _, depth = place()
    if len(sums) == 1:
        firsts, sums = [labels[step * tiles] for step in range(count)], [sums[0].at[step] for step in range(count)]
    else:
        firsts = [labels[(depth ^ step) * tiles] for step in range(count)]
    total = jnp.zeros(base.shape, jnp.float32)
    for part in sums:
        for slot in range(SPAN):
            total = total + part[slot].astype(jnp.float32)
    base[...] = phen[row_at(depth * shard + row, height), :].astype(jnp.float32) - total

    def copy(chrom):
        return pltpu.make_async_copy(stage.at[chrom], out.at[chrom, pl.ds(row, height)], done.at[chrom])

    def step(chrom, carry):
        acc[...] = base[...]
        for first, part in zip(firsts, sums):
            slot = chrom - first

            @pl.when((slot >= 0) & (slot < SPAN))
            def _():
                acc[...] += part[slot].astype(jnp.float32)

        stage[chrom] = acc[...].astype(stage.dtype)
        copy(chrom).start()
        return carry

    lax.fori_loop(0, CHROMS, step, 0)

    def finish(chrom, carry):
        copy(chrom).wait()
        return carry

    lax.fori_loop(0, CHROMS, finish, 0)


def leave_out(loco, token, shape, row, height, tiles, count, labels, phen, sums):
    people = phen.shape[1]
    anywhere = pl.BlockSpec(memory_space=pl.ANY)
    specs = [anywhere, pl.BlockSpec(memory_space=pltpu.SMEM)] + [pl.BlockSpec(memory_space=VMEM)] * (1 + len(sums))
    args = [token, labels] + [pltpu.with_memory_space_constraint(a, VMEM) for a in (phen, *sums)]
    before, aliases = 1, {0: 1}
    if loco is not None:
        specs, args, before, aliases = [anywhere] + specs, [loco] + args, 2, {0: 0, 1: 1}

    def body(*refs):
        ins, (out, _, *scratch) = refs[before : len(args)], refs[len(args) :]
        loco_body(row, shape[1], tiles, count, *ins, out, *scratch)

    return pl.pallas_call(
        body,
        out_shape=[jax.ShapeDtypeStruct(shape, jnp.bfloat16), jax.ShapeDtypeStruct(token.shape, token.dtype)],
        in_specs=specs,
        out_specs=[anywhere, anywhere],
        scratch_shapes=[pltpu.VMEM((height, people), jnp.float32)] * 2
        + [pltpu.VMEM((shape[0], height, people), jnp.bfloat16), pltpu.SemaphoreType.DMA((shape[0],))],
        input_output_aliases=aliases,
        cost_estimate=pl.CostEstimate(flops=1, bytes_accessed=1, transcendentals=0),
        compiler_params=pltpu.CompilerParams(vmem_limit_bytes=8 * 2**20),
    )(*args)


def piece_steps(genotypes, estimate, phenotypes, prior_logit, slab_var, noise_var, tile_chrom):
    people_dev, mark_dev = genotypes.shape
    shard = estimate.shape[0]
    mk_count = lax.axis_size("mk")
    people_count = lax.axis_size(("pp", "sub"))
    marker_root = math.sqrt(mark_dev * mk_count)
    people_root = math.sqrt(people_dev * people_count)
    tile_dev = mark_dev // TILE
    swap = [(0, 1), (1, 0)]

    def along(step):
        return [(i, i ^ step) for i in range(mk_count)]

    firsts, row = [], 0
    for part in FIRST:
        firsts.append((row, shard * part // sum(FIRST)))
        row += firsts[-1][1]
    seconds = [(of, firsts[of][1] * a // n, firsts[of][1] * b // n - firsts[of][1] * a // n) for of, a, b, n in SECOND]

    own = [estimate[row : row + height] for row, height in firsts]
    across = [lax.ppermute(one, "pp", swap) for one in own]
    beside = [lax.ppermute(one, "sub", swap) for one in own]
    corner = [lax.ppermute(one, "sub", swap) for one in across]
    spread = slab_var + noise_var
    coefs = jnp.stack(
        [prior_logit + 0.5 * jnp.log(noise_var / spread), 0.5 * (1.0 / noise_var - 1.0 / spread), slab_var / spread],
        axis=1,
    )
    coefs_across = lax.ppermute(coefs, "pp", swap)
    steps, whole, loco = Steps(genotypes), None, None
    before, after = [{} for _ in firsts], [{} for _ in seconds]
    f32, bf16 = jnp.float32, jnp.bfloat16
    for stage, at in ORDER:
        if stage in ("pred", "two", "res"):
            now, (row, height) = before[at], firsts[at]
        else:
            now, (of, low, height) = after[at], seconds[at]
            row = firsts[of][0] + low
        half, wide = (2 * height, people_dev), (2 * height, mark_dev)
        narrow = pltpu.VMEM((2 * height, mark_dev // SPLIT), bf16)
        if stage == "pred":
            keep, send = steps.call(
                predict_body,
                [pltpu.VMEM(half, f32), pltpu.VMEM(half, bf16)],
                args=[own[at], across[at], beside[at], corner[at]],
                streamed=True,
                scratch=[pltpu.VMEM((4 * height, people_dev), f32)],
            )
            now["pred"] = keep, lax.ppermute(send, "mk", along(1))
        elif stage == "two":
            (two,) = steps.call(two_body, [pltpu.VMEM(half, bf16)], args=now["pred"])
            now["two"] = two, lax.ppermute(two, "mk", along(2))
        elif stage == "res":
            body = functools.partial(residual_body, shard, row)
            (residual,) = steps.call(body, [pltpu.VMEM(half, bf16)], args=[phenotypes, *now["two"]])
            now["res"] = residual, lax.ppermute(residual, "mk", along(1))
        elif stage == "score":
            keep, *sends = steps.call(
                functools.partial(score_body, low),
                [pltpu.VMEM(wide, f32)] + [pltpu.VMEM((2 * height, mark_dev // SCORE_SPLIT), bf16)] * SCORE_SPLIT,
                args=before[of]["res"],
                streamed=True,
                after=[coefs_across],
            )
            now["score"] = [keep] + [lax.ppermute(send, "sub", swap) for send in sends]
        elif stage == "chip":
            chip, send = steps.call(chip_body, [pltpu.VMEM(wide, f32), pltpu.VMEM(wide, bf16)], args=now["score"])
            now["chip"] = chip, lax.ppermute(send, "pp", swap)
        elif stage == "den":
            *updated, whole = steps.call(
                functools.partial(denoise_body, marker_root, people_root, low, row),
                [narrow] * SPLIT,
                args=[own[of], across[of], *now["chip"], coefs, coefs_across],
                scratch=[pltpu.SemaphoreType.DMA((SPLIT,))],
                into=whole,
                fresh=None if whole is not None else jax.ShapeDtypeStruct(estimate.shape, estimate.dtype),
            )
            now["den"] = updated + [lax.ppermute(one, "sub", swap) for one in updated]
        elif stage == "chrom":
            block, together = (SPAN, height, people_dev), at in TOGETHER
            sums = steps.call(
                functools.partial(chrom_body, together),
                [pltpu.VMEM((mk_count, *block), bf16)] if together else [pltpu.VMEM(block, bf16)] * mk_count,
                [tile_chrom],
                now["den"],
                streamed=True,
                scratch=[pltpu.VMEM((4 * height, people_dev), f32)],
                after=[after[at - 1]["chrom"][2]] if at and HOLD else [],
            )
            if together:
                now["chrom"] = [lax.all_to_all(sums[0], "mk", 0, 0, tiled=True)]
            else:
                now["chrom"] = [sums[0]] + [lax.ppermute(sums[step], "mk", along(step)) for step in range(1, mk_count)]
        else:
            shape = (CHROMS, shard, people_dev)
            loco, token = leave_out(
                loco, steps.token, shape, row, height, tile_dev, mk_count, tile_chrom, phenotypes, now["chrom"]
            )
            if CHAIN:
                steps.token = token
    return (whole, loco)


def solution(mesh):
    placed = (
        P(("grp", "pp", "sub"), "mk"),
        P(("grp", "pp", "sub"), "mk"),
        P("grp", ("pp", "sub")),
        P(("grp", "pp", "sub")),
        P(("grp", "pp", "sub")),
        P(("grp", "pp", "sub")),
        P("grp"),
    )
    by_pieces = (mesh.shape["pp"], mesh.shape["sub"], mesh.shape["mk"]) == (2, 2, 4)
    return jax.shard_map(
        piece_steps if by_pieces else whole_mesh_steps,
        mesh=mesh,
        in_specs=placed,
        out_specs=(P(("grp", "pp", "sub"), "mk"), P("grp", "mk", ("pp", "sub"))),
        check_vma=False,
    )
```

```python
import functools
import math

import jax
import jax.numpy as jnp
from jax import lax
from jax.experimental import pallas as pl
from jax.experimental.pallas import tpu as pltpu
from jax.sharding import PartitionSpec as P

CHROMS = 22
TILE = 512
SPAN = 6
LOADS = 2
SPLIT = 4
SCORE_SPLIT = 8
TOGETHER = ()
CHAIN = True
RESIDENT = True
TOUCH = False
OPEN = True
REUSE = True
STAGGER = False
TOUCHED = ()
CROSS = (2, 2)
TRAVEL = (1, 1)
DENOISE = ((1, 2), (2, 2))
LIMIT = 4
HOLD = True
HOLD_CHIP = False
FIRST = (1, 1)
SECOND = ((0, 0, 1, 1), (1, 0, 1, 1))
ORDER = (('pred', 0), ('two', 0), ('pass', 1), ('pred', 1), ('res', 0), ('two', 1), ('score', 0), ('res', 1), ('chip', 0), ('score', 1), ('chip', 1), ('den', 0), ('chrom', 0), ('den', 1), ('chrom', 1), ('leave', 0), ('leave', 1))


def denoise(estimate, scores, prior_logit, slab_var, noise_var, marker_root, people_root):
    observed = marker_root * estimate.astype(jnp.float32) + scores * (1.0 / people_root)
    slab_col = slab_var[:, None]
    noise_col = noise_var[:, None]
    spread = slab_col + noise_col
    log_odds = (
        prior_logit[:, None]
        + 0.5 * jnp.log(noise_col / spread)
        + 0.5 * observed * observed * (1.0 / noise_col - 1.0 / spread)
    )
    posterior = jax.nn.sigmoid(log_odds) * (slab_col / spread) * observed
    return (posterior * (1.0 / marker_root)).astype(jnp.bfloat16)


def whole_mesh_steps(genotypes, estimate, phenotypes, prior_logit, slab_var, noise_var, tile_chrom):
    people_dev, mark_dev = genotypes.shape
    mk_count = lax.axis_size("mk")
    people_count = lax.axis_size(("pp", "sub"))
    traits = phenotypes.shape[0]
    partial_pred = lax.dot_general(
        lax.all_gather(estimate, ("pp", "sub"), axis=0, tiled=True),
        genotypes,
        (((1,), (1,)), ((), ())),
        preferred_element_type=jnp.float32,
    )
    share_rows = traits // mk_count
    offset = lax.axis_index("mk") * share_rows
    phen_share = lax.dynamic_slice_in_dim(phenotypes, offset, share_rows, 0).astype(jnp.float32)
    prediction = lax.psum(partial_pred, "mk")
    residual = (phenotypes.astype(jnp.float32) - prediction).astype(jnp.bfloat16)
    scores = lax.psum_scatter(
        jnp.dot(residual, genotypes, preferred_element_type=jnp.float32),
        ("pp", "sub"),
        scatter_dimension=0,
        tiled=True,
    )
    updated = denoise(
        estimate,
        scores,
        prior_logit,
        slab_var,
        noise_var,
        math.sqrt(mark_dev * mk_count),
        math.sqrt(people_dev * people_count),
    )
    tile_dev = mark_dev // TILE
    own_tiles = lax.dynamic_slice_in_dim(tile_chrom, lax.axis_index("mk") * tile_dev, tile_dev, 0)
    labels = own_tiles[0] + jnp.arange(SPAN, dtype=jnp.int32)
    member = (labels[:, None] == own_tiles[None, :]).astype(jnp.float32)
    geno_tiles = genotypes.reshape(people_dev, tile_dev, TILE)
    shard_rows = lax.all_gather(updated, ("pp", "sub"), axis=0, tiled=True)
    tile_terms = jnp.einsum(
        "kta,pta->tkp",
        shard_rows.reshape(shard_rows.shape[0], tile_dev, TILE),
        geno_tiles,
        preferred_element_type=jnp.float32,
    )
    local_sums = jnp.einsum("st,tkp->skp", member, tile_terms, precision=lax.Precision.HIGHEST)
    received = lax.all_to_all(local_sums, "mk", split_axis=1, concat_axis=0, tiled=True)
    firsts = tile_chrom.reshape(mk_count, tile_dev)[:, 0]
    sources = (firsts[:, None] + jnp.arange(SPAN, dtype=jnp.int32)[None, :]).reshape(-1)
    assign = (jnp.arange(CHROMS, dtype=jnp.int32)[:, None] == sources[None, :]).astype(jnp.float32)
    chrom_sums = jnp.einsum("cj,jkp->ckp", assign, received, precision=lax.Precision.HIGHEST)
    combined = jnp.sum(chrom_sums, axis=0)
    loco_out = (phen_share[None] - combined[None] + chrom_sums).astype(jnp.bfloat16)
    return (updated, loco_out)


VMEM = pltpu.MemorySpace.VMEM
NT = (((1,), (1,)), ((), ()))


class Steps:
    def __init__(self, genotypes):
        self.genotypes = genotypes
        self.token = jnp.zeros((8, 128), jnp.float32)

    def call(self, body, outs, scalars=(), args=(), streamed=False, scratch=(), after=(), into=None, fresh=None, touch=False, reuse=False):
        geno = self.genotypes
        tiles = geno.shape[1] // TILE
        given = streamed or TOUCH or touch
        after = list(after) + [into] * (into is not None)
        skip = 1 + len(after)
        filled = [fresh] * (fresh is not None) + [jax.ShapeDtypeStruct(one.shape, one.dtype) for one in [into] * (into is not None)]
        count = skip + len(scalars) + len(args)

        def kernel(*refs):
            ins, rest = list(refs[skip:count]), list(refs[count:])
            if given and not streamed:
                rest.pop(0)
            if streamed and RESIDENT:
                ins += [rest.pop(0), lambda tile: None]
            elif streamed:
                source = rest.pop(0)
                held, arrived = rest[1 + len(outs) : 3 + len(outs)]
                del rest[1 + len(outs) : 3 + len(outs)]
                copies = []
                for part in range(LOADS):
                    columns = pl.ds(part * geno.shape[1] // LOADS, geno.shape[1] // LOADS)
                    copies.append(pltpu.make_async_copy(source.at[:, columns], held.at[:, columns], arrived.at[part]))
                for copy in copies:
                    copy.start()

                def need(tile):
                    if tile * LOADS % tiles == 0:
                        copies[tile * LOADS // tiles].wait()

                ins += [held, need]
            body(*ins, *rest[1:])

        anywhere = pl.BlockSpec(memory_space=pl.ANY)
        stream_scratch = [pltpu.VMEM(geno.shape, geno.dtype), pltpu.SemaphoreType.DMA((LOADS,))] if streamed and not RESIDENT else []
        token, *results = pl.pallas_call(
            kernel,
            out_shape=[jax.ShapeDtypeStruct(self.token.shape, self.token.dtype), *outs, *filled],
            in_specs=[anywhere] * skip
            + [pl.BlockSpec(memory_space=pltpu.SMEM)] * len(scalars)
            + [pl.BlockSpec(memory_space=VMEM)] * len(args)
            + [pl.BlockSpec(memory_space=VMEM) if RESIDENT else anywhere] * given,
            out_specs=[anywhere] + [pl.BlockSpec(memory_space=VMEM)] * len(outs) + [anywhere] * len(filled),
            scratch_shapes=stream_scratch + list(scratch),
            input_output_aliases={0: 0}
            | ({} if into is None else {skip - 1: 1 + len(outs)})
            | ({skip + len(scalars): 1} if reuse else {}),
            cost_estimate=pl.CostEstimate(flops=1, bytes_accessed=1, transcendentals=0),
            compiler_params=pltpu.CompilerParams(vmem_limit_bytes=LIMIT * 2**20),
        )(self.token, *after, *scalars, *[pltpu.with_memory_space_constraint(a, VMEM) for a in args], *[pltpu.with_memory_space_constraint(geno, VMEM if RESIDENT else pltpu.MemorySpace.HBM)] * given)
        if CHAIN:
            self.token = token
        return results


def columns_of(tile):
    return slice(tile * TILE, (tile + 1) * TILE)


def place():
    return lax.axis_index("pp") * 2 + lax.axis_index("sub"), lax.axis_index("mk")


def row_at(start, height):
    return pl.ds(pl.multiple_of(start, 16), height)


def piece_of(refs, tile):
    for ref in refs:
        if tile < ref.shape[1] // TILE:
            return ref, columns_of(tile)
        tile -= ref.shape[1] // TILE


def copy_body(*refs):
    count = len(refs) // 2
    for source, target in zip(refs[:count], refs[count:]):
        target[...] = source[...]


def open_body(source, prior_logit, slab_var, noise_var, target, coefs):
    target[...] = source[...]
    slab, noise = slab_var[...], noise_var[...]
    spread = slab + noise
    base = prior_logit[...] + 0.5 * jnp.log(noise / spread)
    curve = 0.5 * (1.0 / noise - 1.0 / spread)
    shard = slab.shape[1]
    here = lax.broadcasted_iota(jnp.int32, (shard, shard), 0) == lax.broadcasted_iota(jnp.int32, (shard, shard), 1)
    lane = lax.broadcasted_iota(jnp.int32, coefs.shape, 1)
    value = jnp.zeros(coefs.shape, jnp.float32)
    for at, row in enumerate((base, curve, slab / spread)):
        column = jnp.sum(jnp.where(here, jnp.broadcast_to(row, here.shape), 0.0), axis=1, keepdims=True)
        value = jnp.where(lane == at, column, value)
    coefs[...] = value


def predict_body(parts, *refs):
    blocks, (geno, need, keep, send, product) = refs[: 4 * parts], refs[4 * parts :]
    odd = place()[1] % 2
    half = keep.shape[0]
    for tile in range(geno.shape[1] // TILE):
        part = columns_of(tile)
        rows = jnp.concatenate([ref[:, part] for ref in blocks], axis=0)
        need(tile)
        term = lax.dot_general(rows, geno[:, part], NT, preferred_element_type=jnp.float32)
        product[...] = term if tile == 0 else product[...] + term
    keep[...] = product[row_at(odd * half, half), :]
    send[...] = product[row_at(half - odd * half, half), :].astype(send.dtype)


def two_body(keep, came, two):
    two[...] = (keep[...] + came[...].astype(jnp.float32)).astype(two.dtype)


def residual_body(shard, low, phen, two, came, residual):
    me, depth = place()
    height = two.shape[0] // 2
    for block in range(2):
        at = slice(block * height, (block + 1) * height)
        prediction = two[at, :].astype(jnp.float32) + came[at, :].astype(jnp.float32)
        start = (me ^ (depth % 2) ^ (2 * block)) * shard + low
        measured = phen[row_at(start, height), :].astype(jnp.float32)
        residual[at, :] = (measured - prediction).astype(residual.dtype)


def score_body(low, mine, other, geno, need, keep, *sends):
    even = place()[1] % 2 == 0
    half = keep.shape[0]
    height, block = half // 2, mine.shape[0] // 2

    def rows_of(ref):
        return jnp.concatenate([ref[low : low + height], ref[block + low : block + low + height]], axis=0)

    first = jnp.where(even, rows_of(mine), rows_of(other))
    second = jnp.where(even, rows_of(other), rows_of(mine))
    rows = jnp.concatenate([first, second], axis=0)
    for tile in range(geno.shape[1] // TILE):
        part = columns_of(tile)
        need(tile)
        product = jnp.dot(rows, geno[:, part], preferred_element_type=jnp.float32)
        keep[:, part] = product[:half]
        send, inner = piece_of(sends, tile)
        send[:, inner] = product[half:].astype(send.dtype)


def chip_body(keep, *refs):
    came, chip, sends = refs[:SCORE_SPLIT], refs[SCORE_SPLIT], refs[SCORE_SPLIT + 1 :]
    height = keep.shape[0] // 2
    for tile in range(keep.shape[1] // TILE):
        part = columns_of(tile)
        ref, inner = piece_of(came, tile)
        total = keep[:, part] + ref[:, inner].astype(jnp.float32)
        chip[:, part] = total
        send, inner = piece_of(sends, tile)
        send[:height, inner] = total[height:].astype(send.dtype)
        send[height:, inner] = total[:height].astype(send.dtype)


def denoise_body(marker_root, people_root, low, first, begin, parts, pieces, *refs):
    own, across, (coefs, coefs_across, chip, *refs) = refs[:pieces], refs[pieces : 2 * pieces], refs[2 * pieces :]
    came, updated, (whole, stored) = refs[:parts], refs[parts:-2], refs[-2:]
    height = updated[0].shape[0] // 2
    at = slice(low, low + height)
    coef = jnp.concatenate([coefs[first : first + height], coefs_across[first : first + height]], axis=0)
    base, curve, gain = coef[:, 0:1], coef[:, 1:2], coef[:, 2:3]
    width = updated[0].shape[1]
    for tile in range(len(updated) * width // TILE):
        part = columns_of(begin + tile)
        other, inner = piece_of(came, tile)
        scores = chip[:, part] + other[:, inner].astype(jnp.float32)
        blocks = [jnp.concatenate([ref[:, part] for ref in block], axis=0)[at] for block in (own, across)]
        estimate = jnp.concatenate(blocks, axis=0).astype(jnp.float32)
        observed = marker_root * estimate + scores * (1.0 / people_root)
        log_odds = base + curve * observed * observed
        posterior = jax.nn.sigmoid(log_odds) * gain * observed
        ref, inner = piece_of(updated, tile)
        ref[:, inner] = (posterior * (1.0 / marker_root)).astype(ref.dtype)
    copies = []
    for at, ref in enumerate(updated):
        target = whole.at[pl.ds(first, height), pl.ds(begin * TILE + at * width, width)]
        copies.append(pltpu.make_async_copy(ref.at[pl.ds(0, height)], target, stored.at[at]))
    for copy in copies:
        copy.start()
    for copy in copies:
        copy.wait()


def chrom_body(together, pieces, labels, *refs):
    own, beside, (geno, need, *outs, acc) = refs[:pieces], refs[pieces : 2 * pieces], refs[2 * pieces :]
    if together:
        outs = [outs[0].at[to] for to in range(outs[0].shape[0])]
    me, depth = place()
    height = own[0].shape[0] // 2
    base = depth * (geno.shape[1] // TILE)
    starts = []
    for to in range(len(outs)):
        bits = me ^ to if together else me ^ depth ^ to
        starts.append(((bits % 2) * 2 + bits // 2) * height)
    for out in outs:
        out[...] = jnp.zeros(out.shape, out.dtype)
    for tile in range(geno.shape[1] // TILE):
        part = columns_of(tile)
        halves = [ref[:, inner] for ref, inner in (piece_of(own, tile), piece_of(beside, tile))]
        rows = jnp.concatenate(halves, axis=0)
        need(tile)
        product = lax.dot_general(rows, geno[:, part], NT, preferred_element_type=jnp.float32)
        if tile == 0:
            acc[...] = product
        else:
            same = (labels[base + tile] == labels[base + tile - 1]).astype(jnp.float32)
            acc[...] = acc[...] * same + product
        slot = labels[base + tile] - labels[base]
        for start, out in zip(starts, outs):
            out[slot] = acc[row_at(start, height), :].astype(out.dtype)


def loco_body(row, shard, tiles, count, labels, phen, *refs):
    *sums, out, base, stage, done = refs
    height = base.shape[0]
    _, depth = place()
    if len(sums) == 1:
        firsts, sums = [labels[step * tiles] for step in range(count)], [sums[0].at[step] for step in range(count)]
    else:
        firsts = [labels[(depth ^ step) * tiles] for step in range(count)]
    total = jnp.zeros(base.shape, jnp.float32)
    for part in sums:
        for slot in range(SPAN):
            total = total + part[slot].astype(jnp.float32)
    base[...] = phen[row_at(depth * shard + row, height), :].astype(jnp.float32) - total

    def copy(chrom):
        return pltpu.make_async_copy(stage.at[chrom], out.at[chrom, pl.ds(row, height)], done.at[chrom])

    for chrom in range(CHROMS):
        value = base[...]
        for first, part in zip(firsts, sums):
            slot = chrom - first
            inside = ((slot >= 0) & (slot < SPAN)).astype(jnp.float32)
            value = value + inside * part[jnp.clip(slot, 0, SPAN - 1)].astype(jnp.float32)
        stage[chrom] = value.astype(stage.dtype)
        copy(chrom).start()

    def finish(chrom, carry):
        copy(chrom).wait()
        return carry

    lax.fori_loop(0, CHROMS, finish, 0)


def leave_out(loco, token, shape, row, height, tiles, count, labels, phen, sums):
    people = phen.shape[1]
    anywhere = pl.BlockSpec(memory_space=pl.ANY)
    specs = [anywhere, pl.BlockSpec(memory_space=pltpu.SMEM)] + [pl.BlockSpec(memory_space=VMEM)] * (1 + len(sums))
    args = [token, labels] + [pltpu.with_memory_space_constraint(a, VMEM) for a in (phen, *sums)]
    before, aliases = 1, {0: 1}
    if loco is not None:
        specs, args, before, aliases = [anywhere] + specs, [loco] + args, 2, {0: 0, 1: 1}

    def body(*refs):
        ins, (out, _, *scratch) = refs[before : len(args)], refs[len(args) :]
        loco_body(row, shape[1], tiles, count, *ins, out, *scratch)

    return pl.pallas_call(
        body,
        out_shape=[jax.ShapeDtypeStruct(shape, jnp.bfloat16), jax.ShapeDtypeStruct(token.shape, token.dtype)],
        in_specs=specs,
        out_specs=[anywhere, anywhere],
        scratch_shapes=[pltpu.VMEM((height, people), jnp.float32)]
        + [pltpu.VMEM((shape[0], height, people), jnp.bfloat16), pltpu.SemaphoreType.DMA((shape[0],))],
        input_output_aliases=aliases,
        cost_estimate=pl.CostEstimate(flops=1, bytes_accessed=1, transcendentals=0),
        compiler_params=pltpu.CompilerParams(vmem_limit_bytes=8 * 2**20),
    )(*args)


def piece_steps(genotypes, estimate, phenotypes, prior_logit, slab_var, noise_var, tile_chrom):
    people_dev, mark_dev = genotypes.shape
    shard = estimate.shape[0]
    mk_count = lax.axis_size("mk")
    people_count = lax.axis_size(("pp", "sub"))
    marker_root = math.sqrt(mark_dev * mk_count)
    people_root = math.sqrt(people_dev * people_count)
    tile_dev = mark_dev // TILE
    swap = [(0, 1), (1, 0)]

    def along(step):
        return [(i, i ^ step) for i in range(mk_count)]

    firsts, row = [], 0
    for part in FIRST:
        firsts.append((row, shard * part // sum(FIRST)))
        row += firsts[-1][1]
    seconds = [(of, firsts[of][1] * a // n, firsts[of][1] * b // n - firsts[of][1] * a // n) for of, a, b, n in SECOND]

    own = []
    for (row, height), count in zip(firsts, TRAVEL):
        each = height // count
        own.append([estimate[row + at * each : row + at * each + each] for at in range(count)])
    steps, whole, loco = Steps(genotypes), None, None
    across = [[lax.ppermute(one, "pp", swap) for one in own[0]]]
    mirror = [list(ones) for ones in own]
    mirror[0][0], coefs = steps.call(
        open_body,
        [pltpu.VMEM(own[0][0].shape, estimate.dtype), pltpu.VMEM((shard, 128), jnp.float32)],
        args=[own[0][0], *[one.reshape(1, shard) for one in (prior_logit, slab_var, noise_var)]],
        touch=True,
    )
    coefs_across = lax.ppermute(coefs, "pp", swap)
    for ones in own[1:]:
        if STAGGER:
            ones[0] = steps.call(copy_body, [pltpu.VMEM(ones[0].shape, estimate.dtype)], args=ones[:1], after=across[0])[0]
        across.append([lax.ppermute(one, "pp", swap) for one in ones])
    beside = [[lax.ppermute(one, "sub", swap) for one in ones] for ones in mirror]
    corner = [[lax.ppermute(one, "sub", swap) for one in across[0]]] + [None] * (len(across) - 1)
    before, after = [{} for _ in firsts], [{} for _ in seconds]
    f32, bf16 = jnp.float32, jnp.bfloat16
    for stage, at in ORDER:
        if stage == "pass":
            shapes = [pltpu.VMEM(one.shape, one.dtype) for one in across[at]]
            corner[at] = [lax.ppermute(one, "sub", swap) for one in steps.call(copy_body, shapes, args=across[at], after=[coefs_across])]
            continue
        if stage in ("pred", "two", "res"):
            now, (row, height) = before[at], firsts[at]
        else:
            now, (of, low, height) = after[at], seconds[at]
            row = firsts[of][0] + low
        half, wide = (2 * height, people_dev), (2 * height, mark_dev)
        if stage == "pred":
            keep, send = steps.call(
                functools.partial(predict_body, len(own[at])),
                [pltpu.VMEM(half, f32), pltpu.VMEM(half, bf16)],
                args=own[at] + across[at] + beside[at] + corner[at],
                streamed=True,
                scratch=[pltpu.VMEM((4 * height, people_dev), f32)],
            )
            now["pred"] = keep, lax.ppermute(send, "mk", along(1))
        elif stage == "two":
            (two,) = steps.call(two_body, [pltpu.VMEM(half, bf16)], args=now["pred"])
            now["two"] = two, lax.ppermute(two, "mk", along(2))
        elif stage == "res":
            body = functools.partial(residual_body, shard, row)
            (residual,) = steps.call(body, [pltpu.VMEM(half, bf16)], args=[phenotypes, *now["two"]], touch=at in TOUCHED)
            now["res"] = residual, lax.ppermute(residual, "mk", along(1))
        elif stage == "score":
            keep, *sends = steps.call(
                functools.partial(score_body, low),
                [pltpu.VMEM(wide, f32)] + [pltpu.VMEM((2 * height, mark_dev // SCORE_SPLIT), bf16)] * SCORE_SPLIT,
                args=before[of]["res"],
                streamed=True,
            )
            now["score"] = [keep] + [lax.ppermute(send, "sub", swap) for send in sends]
        elif stage == "chip":
            held = [after[at - 1]["chip"][1]] if at and CROSS[at - 1] > 1 and HOLD_CHIP else []
            parts = [pltpu.VMEM((2 * height, mark_dev // CROSS[at]), bf16)] * CROSS[at]
            chip, *sends = steps.call(chip_body, [pltpu.VMEM(wide, f32), *parts], args=now["score"], after=held, reuse=REUSE)
            now["chip"] = [chip] + [lax.ppermute(send, "pp", swap) for send in sends]
        elif stage == "den":
            chip, *came = now["chip"]
            shares = DENOISE[at] if len(came) > 1 else (SPLIT,)
            per, tiles = len(came) // len(shares), tile_dev // len(shares)
            ours, theirs = [], []
            for share, pieces in enumerate(shares):
                *updated, whole = steps.call(
                    functools.partial(denoise_body, marker_root, people_root, low, row, share * tiles, per, len(own[of])),
                    [pltpu.VMEM((2 * height, tiles * TILE // pieces), bf16)] * pieces,
                    args=[*own[of], *across[of], coefs, coefs_across, chip, *came[share * per : (share + 1) * per]],
                    scratch=[pltpu.SemaphoreType.DMA((pieces,))],
                    into=whole,
                    fresh=None if whole is not None else jax.ShapeDtypeStruct(estimate.shape, estimate.dtype),
                )
                ours += updated
                theirs += [lax.ppermute(one, "sub", swap) for one in updated]
            now["den"] = ours + theirs
        elif stage == "chrom":
            block, together = (SPAN, height, people_dev), at in TOGETHER
            sums = steps.call(
                functools.partial(chrom_body, together, len(now["den"]) // 2),
                [pltpu.VMEM((mk_count, *block), bf16)] if together else [pltpu.VMEM(block, bf16)] * mk_count,
                [tile_chrom],
                now["den"],
                streamed=True,
                scratch=[pltpu.VMEM((4 * height, people_dev), f32)],
                after=[after[at - 1]["chrom"][2]] if at and HOLD else [],
            )
            if together:
                now["chrom"] = [lax.all_to_all(sums[0], "mk", 0, 0, tiled=True)]
            else:
                now["chrom"] = [sums[0]] + [lax.ppermute(sums[step], "mk", along(step)) for step in range(1, mk_count)]
        else:
            shape = (CHROMS, shard, people_dev)
            loco, token = leave_out(
                loco, steps.token, shape, row, height, tile_dev, mk_count, tile_chrom, phenotypes, now["chrom"]
            )
            if CHAIN:
                steps.token = token
    return (whole, loco)


def solution(mesh):
    placed = (
        P(("grp", "pp", "sub"), "mk"),
        P(("grp", "pp", "sub"), "mk"),
        P("grp", ("pp", "sub")),
        P(("grp", "pp", "sub")),
        P(("grp", "pp", "sub")),
        P(("grp", "pp", "sub")),
        P("grp"),
    )
    by_pieces = (mesh.shape["pp"], mesh.shape["sub"], mesh.shape["mk"]) == (2, 2, 4)
    return jax.shard_map(
        piece_steps if by_pieces else whole_mesh_steps,
        mesh=mesh,
        in_specs=placed,
        out_specs=(P(("grp", "pp", "sub"), "mk"), P("grp", "mk", ("pp", "sub"))),
        check_vma=False,
    )
```

```python
import functools
import math

import jax
import jax.numpy as jnp
from jax import lax
from jax.experimental import pallas as pl
from jax.experimental.pallas import tpu as pltpu
from jax.sharding import PartitionSpec as P

CHROMS = 22
TILE = 512
SPAN = 6
LOADS = 2
SPLIT = 4
SCORE_SPLIT = 8
TOGETHER = ()
CHAIN = True
RESIDENT = True
TOUCH = False
OPEN = True
REUSE = True
STAGGER = False
TOUCHED = ()
CROSS = (2, 2)
TRAVEL = (1, 1)
DENOISE = ((1, 2), (2, 2))
LIMIT = 4
HOLD = True
HOLD_CHIP = False
FIRST = (1, 1)
SECOND = ((0, 0, 1, 1), (1, 0, 1, 1))
ORDER = (('pred', 0), ('two', 0), ('pass', 1), ('pred', 1), ('res', 0), ('two', 1), ('score', 0), ('res', 1), ('chip', 0), ('score', 1), ('chip', 1), ('den', 0), ('chrom', 0), ('den', 1), ('chrom', 1), ('leave', 0), ('store', 0), ('store', 1), ('leave', 1))


def denoise(estimate, scores, prior_logit, slab_var, noise_var, marker_root, people_root):
    observed = marker_root * estimate.astype(jnp.float32) + scores * (1.0 / people_root)
    slab_col = slab_var[:, None]
    noise_col = noise_var[:, None]
    spread = slab_col + noise_col
    log_odds = (
        prior_logit[:, None]
        + 0.5 * jnp.log(noise_col / spread)
        + 0.5 * observed * observed * (1.0 / noise_col - 1.0 / spread)
    )
    posterior = jax.nn.sigmoid(log_odds) * (slab_col / spread) * observed
    return (posterior * (1.0 / marker_root)).astype(jnp.bfloat16)


def whole_mesh_steps(genotypes, estimate, phenotypes, prior_logit, slab_var, noise_var, tile_chrom):
    people_dev, mark_dev = genotypes.shape
    mk_count = lax.axis_size("mk")
    people_count = lax.axis_size(("pp", "sub"))
    traits = phenotypes.shape[0]
    partial_pred = lax.dot_general(
        lax.all_gather(estimate, ("pp", "sub"), axis=0, tiled=True),
        genotypes,
        (((1,), (1,)), ((), ())),
        preferred_element_type=jnp.float32,
    )
    share_rows = traits // mk_count
    offset = lax.axis_index("mk") * share_rows
    phen_share = lax.dynamic_slice_in_dim(phenotypes, offset, share_rows, 0).astype(jnp.float32)
    prediction = lax.psum(partial_pred, "mk")
    residual = (phenotypes.astype(jnp.float32) - prediction).astype(jnp.bfloat16)
    scores = lax.psum_scatter(
        jnp.dot(residual, genotypes, preferred_element_type=jnp.float32),
        ("pp", "sub"),
        scatter_dimension=0,
        tiled=True,
    )
    updated = denoise(
        estimate,
        scores,
        prior_logit,
        slab_var,
        noise_var,
        math.sqrt(mark_dev * mk_count),
        math.sqrt(people_dev * people_count),
    )
    tile_dev = mark_dev // TILE
    own_tiles = lax.dynamic_slice_in_dim(tile_chrom, lax.axis_index("mk") * tile_dev, tile_dev, 0)
    labels = own_tiles[0] + jnp.arange(SPAN, dtype=jnp.int32)
    member = (labels[:, None] == own_tiles[None, :]).astype(jnp.float32)
    geno_tiles = genotypes.reshape(people_dev, tile_dev, TILE)
    shard_rows = lax.all_gather(updated, ("pp", "sub"), axis=0, tiled=True)
    tile_terms = jnp.einsum(
        "kta,pta->tkp",
        shard_rows.reshape(shard_rows.shape[0], tile_dev, TILE),
        geno_tiles,
        preferred_element_type=jnp.float32,
    )
    local_sums = jnp.einsum("st,tkp->skp", member, tile_terms, precision=lax.Precision.HIGHEST)
    received = lax.all_to_all(local_sums, "mk", split_axis=1, concat_axis=0, tiled=True)
    firsts = tile_chrom.reshape(mk_count, tile_dev)[:, 0]
    sources = (firsts[:, None] + jnp.arange(SPAN, dtype=jnp.int32)[None, :]).reshape(-1)
    assign = (jnp.arange(CHROMS, dtype=jnp.int32)[:, None] == sources[None, :]).astype(jnp.float32)
    chrom_sums = jnp.einsum("cj,jkp->ckp", assign, received, precision=lax.Precision.HIGHEST)
    combined = jnp.sum(chrom_sums, axis=0)
    loco_out = (phen_share[None] - combined[None] + chrom_sums).astype(jnp.bfloat16)
    return (updated, loco_out)


VMEM = pltpu.MemorySpace.VMEM
NT = (((1,), (1,)), ((), ()))


class Steps:
    def __init__(self, genotypes):
        self.genotypes = genotypes
        self.token = jnp.zeros((8, 128), jnp.float32)

    def call(self, body, outs, scalars=(), args=(), streamed=False, scratch=(), after=(), into=None, fresh=None, touch=False, reuse=False):
        geno = self.genotypes
        tiles = geno.shape[1] // TILE
        given = streamed or TOUCH or touch
        after = list(after) + [into] * (into is not None)
        skip = 1 + len(after)
        filled = [fresh] * (fresh is not None) + [jax.ShapeDtypeStruct(one.shape, one.dtype) for one in [into] * (into is not None)]
        count = skip + len(scalars) + len(args)

        def kernel(*refs):
            ins, rest = list(refs[skip:count]), list(refs[count:])
            if given and not streamed:
                rest.pop(0)
            if streamed and RESIDENT:
                ins += [rest.pop(0), lambda tile: None]
            elif streamed:
                source = rest.pop(0)
                held, arrived = rest[1 + len(outs) : 3 + len(outs)]
                del rest[1 + len(outs) : 3 + len(outs)]
                copies = []
                for part in range(LOADS):
                    columns = pl.ds(part * geno.shape[1] // LOADS, geno.shape[1] // LOADS)
                    copies.append(pltpu.make_async_copy(source.at[:, columns], held.at[:, columns], arrived.at[part]))
                for copy in copies:
                    copy.start()

                def need(tile):
                    if tile * LOADS % tiles == 0:
                        copies[tile * LOADS // tiles].wait()

                ins += [held, need]
            body(*ins, *rest[1:])

        anywhere = pl.BlockSpec(memory_space=pl.ANY)
        stream_scratch = [pltpu.VMEM(geno.shape, geno.dtype), pltpu.SemaphoreType.DMA((LOADS,))] if streamed and not RESIDENT else []
        token, *results = pl.pallas_call(
            kernel,
            out_shape=[jax.ShapeDtypeStruct(self.token.shape, self.token.dtype), *outs, *filled],
            in_specs=[anywhere] * skip
            + [pl.BlockSpec(memory_space=pltpu.SMEM)] * len(scalars)
            + [pl.BlockSpec(memory_space=VMEM)] * len(args)
            + [pl.BlockSpec(memory_space=VMEM) if RESIDENT else anywhere] * given,
            out_specs=[anywhere] + [pl.BlockSpec(memory_space=VMEM)] * len(outs) + [anywhere] * len(filled),
            scratch_shapes=stream_scratch + list(scratch),
            input_output_aliases={0: 0}
            | ({} if into is None else {skip - 1: 1 + len(outs)})
            | ({skip + len(scalars): 1} if reuse else {}),
            cost_estimate=pl.CostEstimate(flops=1, bytes_accessed=1, transcendentals=0),
            compiler_params=pltpu.CompilerParams(vmem_limit_bytes=LIMIT * 2**20),
        )(self.token, *after, *scalars, *[pltpu.with_memory_space_constraint(a, VMEM) for a in args], *[pltpu.with_memory_space_constraint(geno, VMEM if RESIDENT else pltpu.MemorySpace.HBM)] * given)
        if CHAIN:
            self.token = token
        return results


def columns_of(tile):
    return slice(tile * TILE, (tile + 1) * TILE)


def place():
    return lax.axis_index("pp") * 2 + lax.axis_index("sub"), lax.axis_index("mk")


def row_at(start, height):
    return pl.ds(pl.multiple_of(start, 16), height)


def piece_of(refs, tile):
    for ref in refs:
        if tile < ref.shape[1] // TILE:
            return ref, columns_of(tile)
        tile -= ref.shape[1] // TILE


def copy_body(*refs):
    count = len(refs) // 2
    for source, target in zip(refs[:count], refs[count:]):
        target[...] = source[...]


def open_body(source, prior_logit, slab_var, noise_var, target, coefs):
    target[...] = source[...]
    slab, noise = slab_var[...], noise_var[...]
    spread = slab + noise
    base = prior_logit[...] + 0.5 * jnp.log(noise / spread)
    curve = 0.5 * (1.0 / noise - 1.0 / spread)
    shard = slab.shape[1]
    here = lax.broadcasted_iota(jnp.int32, (shard, shard), 0) == lax.broadcasted_iota(jnp.int32, (shard, shard), 1)
    lane = lax.broadcasted_iota(jnp.int32, coefs.shape, 1)
    value = jnp.zeros(coefs.shape, jnp.float32)
    for at, row in enumerate((base, curve, slab / spread)):
        column = jnp.sum(jnp.where(here, jnp.broadcast_to(row, here.shape), 0.0), axis=1, keepdims=True)
        value = jnp.where(lane == at, column, value)
    coefs[...] = value


def predict_body(parts, *refs):
    blocks, (geno, need, keep, send, product) = refs[: 4 * parts], refs[4 * parts :]
    odd = place()[1] % 2
    half = keep.shape[0]
    for tile in range(geno.shape[1] // TILE):
        part = columns_of(tile)
        rows = jnp.concatenate([ref[:, part] for ref in blocks], axis=0)
        need(tile)
        term = lax.dot_general(rows, geno[:, part], NT, preferred_element_type=jnp.float32)
        product[...] = term if tile == 0 else product[...] + term
    keep[...] = product[row_at(odd * half, half), :]
    send[...] = product[row_at(half - odd * half, half), :].astype(send.dtype)


def two_body(keep, came, two):
    two[...] = (keep[...] + came[...].astype(jnp.float32)).astype(two.dtype)


def residual_body(shard, low, phen, two, came, residual):
    me, depth = place()
    height = two.shape[0] // 2
    for block in range(2):
        at = slice(block * height, (block + 1) * height)
        prediction = two[at, :].astype(jnp.float32) + came[at, :].astype(jnp.float32)
        start = (me ^ (depth % 2) ^ (2 * block)) * shard + low
        measured = phen[row_at(start, height), :].astype(jnp.float32)
        residual[at, :] = (measured - prediction).astype(residual.dtype)


def score_body(low, mine, other, geno, need, keep, *sends):
    even = place()[1] % 2 == 0
    half = keep.shape[0]
    height, block = half // 2, mine.shape[0] // 2

    def rows_of(ref):
        return jnp.concatenate([ref[low : low + height], ref[block + low : block + low + height]], axis=0)

    first = jnp.where(even, rows_of(mine), rows_of(other))
    second = jnp.where(even, rows_of(other), rows_of(mine))
    rows = jnp.concatenate([first, second], axis=0)
    for tile in range(geno.shape[1] // TILE):
        part = columns_of(tile)
        need(tile)
        product = jnp.dot(rows, geno[:, part], preferred_element_type=jnp.float32)
        keep[:, part] = product[:half]
        send, inner = piece_of(sends, tile)
        send[:, inner] = product[half:].astype(send.dtype)


def chip_body(keep, *refs):
    came, chip, sends = refs[:SCORE_SPLIT], refs[SCORE_SPLIT], refs[SCORE_SPLIT + 1 :]
    height = keep.shape[0] // 2
    for tile in range(keep.shape[1] // TILE):
        part = columns_of(tile)
        ref, inner = piece_of(came, tile)
        total = keep[:, part] + ref[:, inner].astype(jnp.float32)
        chip[:, part] = total
        send, inner = piece_of(sends, tile)
        send[:height, inner] = total[height:].astype(send.dtype)
        send[height:, inner] = total[:height].astype(send.dtype)


def denoise_body(marker_root, people_root, low, first, begin, parts, pieces, *refs):
    own, across, (coefs, coefs_across, chip, *refs) = refs[:pieces], refs[pieces : 2 * pieces], refs[2 * pieces :]
    came, updated = refs[:parts], refs[parts:]
    height = updated[0].shape[0] // 2
    at = slice(low, low + height)
    coef = jnp.concatenate([coefs[first : first + height], coefs_across[first : first + height]], axis=0)
    base, curve, gain = coef[:, 0:1], coef[:, 1:2], coef[:, 2:3]
    width = updated[0].shape[1]
    for tile in range(len(updated) * width // TILE):
        part = columns_of(begin + tile)
        other, inner = piece_of(came, tile)
        scores = chip[:, part] + other[:, inner].astype(jnp.float32)
        blocks = [jnp.concatenate([ref[:, part] for ref in block], axis=0)[at] for block in (own, across)]
        estimate = jnp.concatenate(blocks, axis=0).astype(jnp.float32)
        observed = marker_root * estimate + scores * (1.0 / people_root)
        log_odds = base + curve * observed * observed
        posterior = jax.nn.sigmoid(log_odds) * gain * observed
        ref, inner = piece_of(updated, tile)
        ref[:, inner] = (posterior * (1.0 / marker_root)).astype(ref.dtype)


def store_body(first, *refs):
    *parts, whole, stored = refs
    copies, begin, height = [], 0, parts[0].shape[0] // 2
    for at, ref in enumerate(parts):
        target = whole.at[pl.ds(first, height), pl.ds(begin, ref.shape[1])]
        copies.append(pltpu.make_async_copy(ref.at[pl.ds(0, height)], target, stored.at[at]))
        copies[-1].start()
        begin += ref.shape[1]
    for copy in copies:
        copy.wait()


def chrom_body(together, pieces, labels, *refs):
    own, beside, (geno, need, *outs, acc) = refs[:pieces], refs[pieces : 2 * pieces], refs[2 * pieces :]
    if together:
        outs = [outs[0].at[to] for to in range(outs[0].shape[0])]
    me, depth = place()
    height = own[0].shape[0] // 2
    base = depth * (geno.shape[1] // TILE)
    starts = []
    for to in range(len(outs)):
        bits = me ^ to if together else me ^ depth ^ to
        starts.append(((bits % 2) * 2 + bits // 2) * height)
    for out in outs:
        out[...] = jnp.zeros(out.shape, out.dtype)
    for tile in range(geno.shape[1] // TILE):
        part = columns_of(tile)
        halves = [ref[:, inner] for ref, inner in (piece_of(own, tile), piece_of(beside, tile))]
        rows = jnp.concatenate(halves, axis=0)
        need(tile)
        product = lax.dot_general(rows, geno[:, part], NT, preferred_element_type=jnp.float32)
        if tile == 0:
            acc[...] = product
        else:
            same = (labels[base + tile] == labels[base + tile - 1]).astype(jnp.float32)
            acc[...] = acc[...] * same + product
        slot = labels[base + tile] - labels[base]
        for start, out in zip(starts, outs):
            out[slot] = acc[row_at(start, height), :].astype(out.dtype)


def loco_body(row, shard, tiles, count, labels, phen, *refs):
    *sums, out, base, stage, done = refs
    height = base.shape[0]
    _, depth = place()
    if len(sums) == 1:
        firsts, sums = [labels[step * tiles] for step in range(count)], [sums[0].at[step] for step in range(count)]
    else:
        firsts = [labels[(depth ^ step) * tiles] for step in range(count)]
    total = jnp.zeros(base.shape, jnp.float32)
    for part in sums:
        for slot in range(SPAN):
            total = total + part[slot].astype(jnp.float32)
    base[...] = phen[row_at(depth * shard + row, height), :].astype(jnp.float32) - total

    group = -(-CHROMS // done.shape[0])
    copies = []
    for chrom in range(CHROMS):
        value = base[...]
        for first, part in zip(firsts, sums):
            slot = chrom - first
            inside = ((slot >= 0) & (slot < SPAN)).astype(jnp.float32)
            value = value + inside * part[jnp.clip(slot, 0, SPAN - 1)].astype(jnp.float32)
        stage[chrom] = value.astype(stage.dtype)
        if (chrom + 1) % group == 0 or chrom + 1 == CHROMS:
            begin = chrom // group * group
            some = pl.ds(begin, chrom + 1 - begin)
            copies.append(pltpu.make_async_copy(stage.at[some], out.at[some, pl.ds(row, height)], done.at[len(copies)]))
            copies[-1].start()
    for copy in copies:
        copy.wait()


def leave_out(loco, token, shape, row, height, tiles, count, labels, phen, sums):
    people = phen.shape[1]
    anywhere = pl.BlockSpec(memory_space=pl.ANY)
    specs = [anywhere, pl.BlockSpec(memory_space=pltpu.SMEM)] + [pl.BlockSpec(memory_space=VMEM)] * (1 + len(sums))
    args = [token, labels] + [pltpu.with_memory_space_constraint(a, VMEM) for a in (phen, *sums)]
    before, aliases = 1, {0: 1}
    if loco is not None:
        specs, args, before, aliases = [anywhere] + specs, [loco] + args, 2, {0: 0, 1: 1}

    def body(*refs):
        ins, (out, _, *scratch) = refs[before : len(args)], refs[len(args) :]
        loco_body(row, shape[1], tiles, count, *ins, out, *scratch)

    return pl.pallas_call(
        body,
        out_shape=[jax.ShapeDtypeStruct(shape, jnp.bfloat16), jax.ShapeDtypeStruct(token.shape, token.dtype)],
        in_specs=specs,
        out_specs=[anywhere, anywhere],
        scratch_shapes=[pltpu.VMEM((height, people), jnp.float32)]
        + [pltpu.VMEM((shape[0], height, people), jnp.bfloat16), pltpu.SemaphoreType.DMA((3,))],
        input_output_aliases=aliases,
        cost_estimate=pl.CostEstimate(flops=1, bytes_accessed=1, transcendentals=0),
        compiler_params=pltpu.CompilerParams(vmem_limit_bytes=8 * 2**20),
    )(*args)


def piece_steps(genotypes, estimate, phenotypes, prior_logit, slab_var, noise_var, tile_chrom):
    people_dev, mark_dev = genotypes.shape
    shard = estimate.shape[0]
    mk_count = lax.axis_size("mk")
    people_count = lax.axis_size(("pp", "sub"))
    marker_root = math.sqrt(mark_dev * mk_count)
    people_root = math.sqrt(people_dev * people_count)
    tile_dev = mark_dev // TILE
    swap = [(0, 1), (1, 0)]

    def along(step):
        return [(i, i ^ step) for i in range(mk_count)]

    firsts, row = [], 0
    for part in FIRST:
        firsts.append((row, shard * part // sum(FIRST)))
        row += firsts[-1][1]
    seconds = [(of, firsts[of][1] * a // n, firsts[of][1] * b // n - firsts[of][1] * a // n) for of, a, b, n in SECOND]

    own = []
    for (row, height), count in zip(firsts, TRAVEL):
        each = height // count
        own.append([estimate[row + at * each : row + at * each + each] for at in range(count)])
    steps, whole, loco = Steps(genotypes), None, None
    across = [[lax.ppermute(one, "pp", swap) for one in own[0]]]
    mirror = [list(ones) for ones in own]
    mirror[0][0], coefs = steps.call(
        open_body,
        [pltpu.VMEM(own[0][0].shape, estimate.dtype), pltpu.VMEM((shard, 128), jnp.float32)],
        args=[own[0][0], *[one.reshape(1, shard) for one in (prior_logit, slab_var, noise_var)]],
        touch=True,
    )
    coefs_across = lax.ppermute(coefs, "pp", swap)
    for ones in own[1:]:
        if STAGGER:
            ones[0] = steps.call(copy_body, [pltpu.VMEM(ones[0].shape, estimate.dtype)], args=ones[:1], after=across[0])[0]
        across.append([lax.ppermute(one, "pp", swap) for one in ones])
    beside = [[lax.ppermute(one, "sub", swap) for one in ones] for ones in mirror]
    corner = [[lax.ppermute(one, "sub", swap) for one in across[0]]] + [None] * (len(across) - 1)
    before, after = [{} for _ in firsts], [{} for _ in seconds]
    f32, bf16 = jnp.float32, jnp.bfloat16
    for stage, at in ORDER:
        if stage == "pass":
            shapes = [pltpu.VMEM(one.shape, one.dtype) for one in across[at]]
            corner[at] = [lax.ppermute(one, "sub", swap) for one in steps.call(copy_body, shapes, args=across[at], after=[coefs_across])]
            continue
        if stage in ("pred", "two", "res"):
            now, (row, height) = before[at], firsts[at]
        else:
            now, (of, low, height) = after[at], seconds[at]
            row = firsts[of][0] + low
        half, wide = (2 * height, people_dev), (2 * height, mark_dev)
        if stage == "pred":
            keep, send = steps.call(
                functools.partial(predict_body, len(own[at])),
                [pltpu.VMEM(half, f32), pltpu.VMEM(half, bf16)],
                args=own[at] + across[at] + beside[at] + corner[at],
                streamed=True,
                scratch=[pltpu.VMEM((4 * height, people_dev), f32)],
            )
            now["pred"] = keep, lax.ppermute(send, "mk", along(1))
        elif stage == "two":
            (two,) = steps.call(two_body, [pltpu.VMEM(half, bf16)], args=now["pred"])
            now["two"] = two, lax.ppermute(two, "mk", along(2))
        elif stage == "res":
            body = functools.partial(residual_body, shard, row)
            (residual,) = steps.call(body, [pltpu.VMEM(half, bf16)], args=[phenotypes, *now["two"]], touch=at in TOUCHED)
            now["res"] = residual, lax.ppermute(residual, "mk", along(1))
        elif stage == "score":
            keep, *sends = steps.call(
                functools.partial(score_body, low),
                [pltpu.VMEM(wide, f32)] + [pltpu.VMEM((2 * height, mark_dev // SCORE_SPLIT), bf16)] * SCORE_SPLIT,
                args=before[of]["res"],
                streamed=True,
            )
            now["score"] = [keep] + [lax.ppermute(send, "sub", swap) for send in sends]
        elif stage == "chip":
            held = [after[at - 1]["chip"][1]] if at and CROSS[at - 1] > 1 and HOLD_CHIP else []
            parts = [pltpu.VMEM((2 * height, mark_dev // CROSS[at]), bf16)] * CROSS[at]
            chip, *sends = steps.call(chip_body, [pltpu.VMEM(wide, f32), *parts], args=now["score"], after=held, reuse=REUSE)
            now["chip"] = [chip] + [lax.ppermute(send, "pp", swap) for send in sends]
        elif stage == "den":
            chip, *came = now["chip"]
            shares = DENOISE[at] if len(came) > 1 else (SPLIT,)
            per, tiles = len(came) // len(shares), tile_dev // len(shares)
            ours, theirs = [], []
            for share, pieces in enumerate(shares):
                updated = steps.call(
                    functools.partial(denoise_body, marker_root, people_root, low, row, share * tiles, per, len(own[of])),
                    [pltpu.VMEM((2 * height, tiles * TILE // pieces), bf16)] * pieces,
                    args=[*own[of], *across[of], coefs, coefs_across, chip, *came[share * per : (share + 1) * per]],
                )
                ours += updated
                theirs += [lax.ppermute(one, "sub", swap) for one in updated]
            now["den"] = ours + theirs
        elif stage == "store":
            mine = now["den"][: len(now["den"]) // 2]
            (whole,) = steps.call(
                functools.partial(store_body, row),
                [],
                args=mine,
                scratch=[pltpu.SemaphoreType.DMA((len(mine),))],
                into=whole,
                fresh=None if whole is not None else jax.ShapeDtypeStruct(estimate.shape, estimate.dtype),
            )
        elif stage == "chrom":
            block, together = (SPAN, height, people_dev), at in TOGETHER
            pieces = len(now["den"]) // 2
            sums = steps.call(
                functools.partial(chrom_body, together, pieces),
                [pltpu.VMEM((mk_count, *block), bf16)] if together else [pltpu.VMEM(block, bf16)] * mk_count,
                [tile_chrom],
                now["den"],
                streamed=True,
                scratch=[pltpu.VMEM((4 * height, people_dev), f32)],
                after=[after[at - 1]["chrom"][2]] if at and HOLD else [],
            )
            if together:
                now["chrom"] = [lax.all_to_all(sums[0], "mk", 0, 0, tiled=True)]
            else:
                now["chrom"] = [sums[0]] + [lax.ppermute(sums[step], "mk", along(step)) for step in range(1, mk_count)]
        else:
            shape = (CHROMS, shard, people_dev)
            loco, token = leave_out(
                loco, steps.token, shape, row, height, tile_dev, mk_count, tile_chrom, phenotypes, now["chrom"]
            )
            if CHAIN:
                steps.token = token
    return (whole, loco)


def solution(mesh):
    placed = (
        P(("grp", "pp", "sub"), "mk"),
        P(("grp", "pp", "sub"), "mk"),
        P("grp", ("pp", "sub")),
        P(("grp", "pp", "sub")),
        P(("grp", "pp", "sub")),
        P(("grp", "pp", "sub")),
        P("grp"),
    )
    by_pieces = (mesh.shape["pp"], mesh.shape["sub"], mesh.shape["mk"]) == (2, 2, 4)
    return jax.shard_map(
        piece_steps if by_pieces else whole_mesh_steps,
        mesh=mesh,
        in_specs=placed,
        out_specs=(P(("grp", "pp", "sub"), "mk"), P("grp", "mk", ("pp", "sub"))),
        check_vma=False,
    )
```

```python
import functools
import math

import jax
import jax.numpy as jnp
from jax import lax
from jax.experimental import pallas as pl
from jax.experimental.pallas import tpu as pltpu
from jax.sharding import PartitionSpec as P

CHROMS = 22
TILE = 512
SPAN = 6
LOADS = 2
SPLIT = 4
SCORE_SPLIT = 8
TOGETHER = ()
CHAIN = True
RESIDENT = True
TOUCH = False
OPEN = True
REUSE = True
STAGGER = False
TOUCHED = ()
CROSS = (2, 2)
TRAVEL = (1, 1)
DENOISE = ((1, 2), (2, 2))
LIMIT = 4
HOLD = True
HOLD_CHIP = False
FIRST = (1, 1)
SECOND = ((0, 0, 1, 1), (1, 0, 1, 1))
ORDER = (('pred', 0), ('two', 0), ('pass', 1), ('pred', 1), ('res', 0), ('two', 1), ('score', 0), ('res', 1), ('chip', 0), ('score', 1), ('chip', 1), ('den', 0), ('chrom', 0), ('den', 1), ('chrom', 1), ('leave', 0), ('store', 0), ('store', 1), ('leave', 1))


def denoise(estimate, scores, prior_logit, slab_var, noise_var, marker_root, people_root):
    observed = marker_root * estimate.astype(jnp.float32) + scores * (1.0 / people_root)
    slab_col = slab_var[:, None]
    noise_col = noise_var[:, None]
    spread = slab_col + noise_col
    log_odds = (
        prior_logit[:, None]
        + 0.5 * jnp.log(noise_col / spread)
        + 0.5 * observed * observed * (1.0 / noise_col - 1.0 / spread)
    )
    posterior = jax.nn.sigmoid(log_odds) * (slab_col / spread) * observed
    return (posterior * (1.0 / marker_root)).astype(jnp.bfloat16)


def whole_mesh_steps(genotypes, estimate, phenotypes, prior_logit, slab_var, noise_var, tile_chrom):
    people_dev, mark_dev = genotypes.shape
    mk_count = lax.axis_size("mk")
    people_count = lax.axis_size(("pp", "sub"))
    traits = phenotypes.shape[0]
    partial_pred = lax.dot_general(
        lax.all_gather(estimate, ("pp", "sub"), axis=0, tiled=True),
        genotypes,
        (((1,), (1,)), ((), ())),
        preferred_element_type=jnp.float32,
    )
    share_rows = traits // mk_count
    offset = lax.axis_index("mk") * share_rows
    phen_share = lax.dynamic_slice_in_dim(phenotypes, offset, share_rows, 0).astype(jnp.float32)
    prediction = lax.psum(partial_pred, "mk")
    residual = (phenotypes.astype(jnp.float32) - prediction).astype(jnp.bfloat16)
    scores = lax.psum_scatter(
        jnp.dot(residual, genotypes, preferred_element_type=jnp.float32),
        ("pp", "sub"),
        scatter_dimension=0,
        tiled=True,
    )
    updated = denoise(
        estimate,
        scores,
        prior_logit,
        slab_var,
        noise_var,
        math.sqrt(mark_dev * mk_count),
        math.sqrt(people_dev * people_count),
    )
    tile_dev = mark_dev // TILE
    own_tiles = lax.dynamic_slice_in_dim(tile_chrom, lax.axis_index("mk") * tile_dev, tile_dev, 0)
    labels = own_tiles[0] + jnp.arange(SPAN, dtype=jnp.int32)
    member = (labels[:, None] == own_tiles[None, :]).astype(jnp.float32)
    geno_tiles = genotypes.reshape(people_dev, tile_dev, TILE)
    shard_rows = lax.all_gather(updated, ("pp", "sub"), axis=0, tiled=True)
    tile_terms = jnp.einsum(
        "kta,pta->tkp",
        shard_rows.reshape(shard_rows.shape[0], tile_dev, TILE),
        geno_tiles,
        preferred_element_type=jnp.float32,
    )
    local_sums = jnp.einsum("st,tkp->skp", member, tile_terms, precision=lax.Precision.HIGHEST)
    received = lax.all_to_all(local_sums, "mk", split_axis=1, concat_axis=0, tiled=True)
    firsts = tile_chrom.reshape(mk_count, tile_dev)[:, 0]
    sources = (firsts[:, None] + jnp.arange(SPAN, dtype=jnp.int32)[None, :]).reshape(-1)
    assign = (jnp.arange(CHROMS, dtype=jnp.int32)[:, None] == sources[None, :]).astype(jnp.float32)
    chrom_sums = jnp.einsum("cj,jkp->ckp", assign, received, precision=lax.Precision.HIGHEST)
    combined = jnp.sum(chrom_sums, axis=0)
    loco_out = (phen_share[None] - combined[None] + chrom_sums).astype(jnp.bfloat16)
    return (updated, loco_out)


VMEM = pltpu.MemorySpace.VMEM
NT = (((1,), (1,)), ((), ()))


class Steps:
    def __init__(self, genotypes):
        self.genotypes = genotypes
        self.token = jnp.zeros((8, 128), jnp.float32)

    def call(self, body, outs, scalars=(), args=(), streamed=False, scratch=(), after=(), into=None, fresh=None, touch=False, reuse=False):
        geno = self.genotypes
        tiles = geno.shape[1] // TILE
        given = streamed or TOUCH or touch
        after = list(after) + [into] * (into is not None)
        skip = 1 + len(after)
        filled = [fresh] * (fresh is not None) + [jax.ShapeDtypeStruct(one.shape, one.dtype) for one in [into] * (into is not None)]
        count = skip + len(scalars) + len(args)

        def kernel(*refs):
            ins, rest = list(refs[skip:count]), list(refs[count:])
            if given and not streamed:
                rest.pop(0)
            if streamed and RESIDENT:
                ins += [rest.pop(0), lambda tile: None]
            elif streamed:
                source = rest.pop(0)
                held, arrived = rest[1 + len(outs) : 3 + len(outs)]
                del rest[1 + len(outs) : 3 + len(outs)]
                copies = []
                for part in range(LOADS):
                    columns = pl.ds(part * geno.shape[1] // LOADS, geno.shape[1] // LOADS)
                    copies.append(pltpu.make_async_copy(source.at[:, columns], held.at[:, columns], arrived.at[part]))
                for copy in copies:
                    copy.start()

                def need(tile):
                    if tile * LOADS % tiles == 0:
                        copies[tile * LOADS // tiles].wait()

                ins += [held, need]
            body(*ins, *rest[1:])

        anywhere = pl.BlockSpec(memory_space=pl.ANY)
        stream_scratch = [pltpu.VMEM(geno.shape, geno.dtype), pltpu.SemaphoreType.DMA((LOADS,))] if streamed and not RESIDENT else []
        token, *results = pl.pallas_call(
            kernel,
            out_shape=[jax.ShapeDtypeStruct(self.token.shape, self.token.dtype), *outs, *filled],
            in_specs=[anywhere] * skip
            + [pl.BlockSpec(memory_space=pltpu.SMEM)] * len(scalars)
            + [pl.BlockSpec(memory_space=VMEM)] * len(args)
            + [pl.BlockSpec(memory_space=VMEM) if RESIDENT else anywhere] * given,
            out_specs=[anywhere] + [pl.BlockSpec(memory_space=VMEM)] * len(outs) + [anywhere] * len(filled),
            scratch_shapes=stream_scratch + list(scratch),
            input_output_aliases={0: 0}
            | ({} if into is None else {skip - 1: 1 + len(outs)})
            | ({skip + len(scalars): 1} if reuse else {}),
            cost_estimate=pl.CostEstimate(flops=1, bytes_accessed=1, transcendentals=0),
            compiler_params=pltpu.CompilerParams(vmem_limit_bytes=LIMIT * 2**20),
        )(self.token, *after, *scalars, *[pltpu.with_memory_space_constraint(a, VMEM) for a in args], *[pltpu.with_memory_space_constraint(geno, VMEM if RESIDENT else pltpu.MemorySpace.HBM)] * given)
        if CHAIN:
            self.token = token
        return results


def columns_of(tile):
    return slice(tile * TILE, (tile + 1) * TILE)


def place():
    return lax.axis_index("pp") * 2 + lax.axis_index("sub"), lax.axis_index("mk")


def row_at(start, height):
    return pl.ds(pl.multiple_of(start, 16), height)


def piece_of(refs, tile):
    for ref in refs:
        if tile < ref.shape[1] // TILE:
            return ref, columns_of(tile)
        tile -= ref.shape[1] // TILE


def copy_body(*refs):
    count = len(refs) // 2
    for source, target in zip(refs[:count], refs[count:]):
        target[...] = source[...]


def open_body(source, prior_logit, slab_var, noise_var, target, coefs):
    target[...] = source[...]
    slab, noise = slab_var[...], noise_var[...]
    spread = slab + noise
    base = prior_logit[...] + 0.5 * jnp.log(noise / spread)
    curve = 0.5 * (1.0 / noise - 1.0 / spread)
    shard = slab.shape[1]
    here = lax.broadcasted_iota(jnp.int32, (shard, shard), 0) == lax.broadcasted_iota(jnp.int32, (shard, shard), 1)
    lane = lax.broadcasted_iota(jnp.int32, coefs.shape, 1)
    value = jnp.zeros(coefs.shape, jnp.float32)
    for at, row in enumerate((base, curve, slab / spread)):
        column = jnp.sum(jnp.where(here, jnp.broadcast_to(row, here.shape), 0.0), axis=1, keepdims=True)
        value = jnp.where(lane == at, column, value)
    coefs[...] = value


def predict_body(parts, *refs):
    blocks, (geno, need, keep, send, product) = refs[: 4 * parts], refs[4 * parts :]
    odd = place()[1] % 2
    half = keep.shape[0]
    for tile in range(geno.shape[1] // TILE):
        part = columns_of(tile)
        rows = jnp.concatenate([ref[:, part] for ref in blocks], axis=0)
        need(tile)
        term = lax.dot_general(rows, geno[:, part], NT, preferred_element_type=jnp.float32)
        product[...] = term if tile == 0 else product[...] + term
    keep[...] = product[row_at(odd * half, half), :]
    send[...] = product[row_at(half - odd * half, half), :].astype(send.dtype)


def two_body(keep, came, two):
    two[...] = (keep[...] + came[...].astype(jnp.float32)).astype(two.dtype)


def residual_body(shard, low, phen, two, came, residual):
    me, depth = place()
    height = two.shape[0] // 2
    for block in range(2):
        at = slice(block * height, (block + 1) * height)
        prediction = two[at, :].astype(jnp.float32) + came[at, :].astype(jnp.float32)
        start = (me ^ (depth % 2) ^ (2 * block)) * shard + low
        measured = phen[row_at(start, height), :].astype(jnp.float32)
        residual[at, :] = (measured - prediction).astype(residual.dtype)


def score_body(low, mine, other, geno, need, keep, *sends):
    even = place()[1] % 2 == 0
    half = keep.shape[0]
    height, block = half // 2, mine.shape[0] // 2

    def rows_of(ref):
        return jnp.concatenate([ref[low : low + height], ref[block + low : block + low + height]], axis=0)

    first = jnp.where(even, rows_of(mine), rows_of(other))
    second = jnp.where(even, rows_of(other), rows_of(mine))
    rows = jnp.concatenate([first, second], axis=0)
    for tile in range(geno.shape[1] // TILE):
        part = columns_of(tile)
        need(tile)
        product = jnp.dot(rows, geno[:, part], preferred_element_type=jnp.float32)
        keep[:, part] = product[:half]
        send, inner = piece_of(sends, tile)
        send[:, inner] = product[half:].astype(send.dtype)


def chip_body(keep, *refs):
    came, chip, sends = refs[:SCORE_SPLIT], refs[SCORE_SPLIT], refs[SCORE_SPLIT + 1 :]
    height = keep.shape[0] // 2
    for tile in range(keep.shape[1] // TILE):
        part = columns_of(tile)
        ref, inner = piece_of(came, tile)
        total = keep[:, part] + ref[:, inner].astype(jnp.float32)
        chip[:, part] = total
        send, inner = piece_of(sends, tile)
        send[:height, inner] = total[height:].astype(send.dtype)
        send[height:, inner] = total[:height].astype(send.dtype)


def denoise_body(marker_root, people_root, low, first, begin, parts, pieces, *refs):
    own, across, (coefs, coefs_across, chip, *refs) = refs[:pieces], refs[pieces : 2 * pieces], refs[2 * pieces :]
    came, updated = refs[:parts], refs[parts:]
    height = updated[0].shape[0] // 2
    at = slice(low, low + height)
    coef = jnp.concatenate([coefs[first : first + height], coefs_across[first : first + height]], axis=0)
    base, curve, gain = coef[:, 0:1], coef[:, 1:2], coef[:, 2:3]
    width = updated[0].shape[1]
    for tile in range(len(updated) * width // TILE):
        part = columns_of(begin + tile)
        other, inner = piece_of(came, tile)
        scores = chip[:, part] + other[:, inner].astype(jnp.float32)
        blocks = [jnp.concatenate([ref[:, part] for ref in block], axis=0)[at] for block in (own, across)]
        estimate = jnp.concatenate(blocks, axis=0).astype(jnp.float32)
        observed = marker_root * estimate + scores * (1.0 / people_root)
        log_odds = base + curve * observed * observed
        posterior = jax.nn.sigmoid(log_odds) * gain * observed
        ref, inner = piece_of(updated, tile)
        ref[:, inner] = (posterior * (1.0 / marker_root)).astype(ref.dtype)


def store_body(first, *refs):
    *parts, whole, stored = refs
    copies, begin, height = [], 0, parts[0].shape[0] // 2
    for at, ref in enumerate(parts):
        target = whole.at[pl.ds(first, height), pl.ds(begin, ref.shape[1])]
        copies.append(pltpu.make_async_copy(ref.at[pl.ds(0, height)], target, stored.at[at]))
        copies[-1].start()
        begin += ref.shape[1]
    for copy in copies:
        copy.wait()


def chrom_body(together, pieces, labels, *refs):
    own, beside, (geno, need, *outs, acc) = refs[:pieces], refs[pieces : 2 * pieces], refs[2 * pieces :]
    if together:
        outs = [outs[0].at[to] for to in range(outs[0].shape[0])]
    me, depth = place()
    height = own[0].shape[0] // 2
    base = depth * (geno.shape[1] // TILE)
    starts = []
    for to in range(len(outs)):
        bits = me ^ to if together else me ^ depth ^ to
        starts.append(((bits % 2) * 2 + bits // 2) * height)
    for out in outs:
        out[...] = jnp.zeros(out.shape, out.dtype)
    for tile in range(geno.shape[1] // TILE):
        part = columns_of(tile)
        halves = [ref[:, inner] for ref, inner in (piece_of(own, tile), piece_of(beside, tile))]
        rows = jnp.concatenate(halves, axis=0)
        need(tile)
        product = lax.dot_general(rows, geno[:, part], NT, preferred_element_type=jnp.float32)
        if tile == 0:
            acc[...] = product
        else:
            same = (labels[base + tile] == labels[base + tile - 1]).astype(jnp.float32)
            acc[...] = acc[...] * same + product
        slot = labels[base + tile] - labels[base]
        for start, out in zip(starts, outs):
            out[slot] = acc[row_at(start, height), :].astype(out.dtype)


def loco_body(row, shard, tiles, count, labels, phen, *refs):
    *sums, out, base, acc, stage, done = refs
    height = base.shape[0]
    _, depth = place()
    if len(sums) == 1:
        firsts, sums = [labels[step * tiles] for step in range(count)], [sums[0].at[step] for step in range(count)]
    else:
        firsts = [labels[(depth ^ step) * tiles] for step in range(count)]
    total = jnp.zeros(base.shape, jnp.float32)
    for part in sums:
        for slot in range(SPAN):
            total = total + part[slot].astype(jnp.float32)
    base[...] = phen[row_at(depth * shard + row, height), :].astype(jnp.float32) - total

    for chrom in range(CHROMS):
        acc[chrom] = base[...]
    for first, part in zip(firsts, sums):
        for slot in range(SPAN):
            chrom = jnp.minimum(first + slot, CHROMS - 1)
            acc[chrom] = acc[chrom] + part[slot].astype(jnp.float32)
    group = -(-CHROMS // done.shape[0])
    copies = []
    for chrom in range(CHROMS):
        stage[chrom] = acc[chrom].astype(stage.dtype)
        if (chrom + 1) % group == 0 or chrom + 1 == CHROMS:
            begin = chrom // group * group
            some = pl.ds(begin, chrom + 1 - begin)
            copies.append(pltpu.make_async_copy(stage.at[some], out.at[some, pl.ds(row, height)], done.at[len(copies)]))
            copies[-1].start()
    for copy in copies:
        copy.wait()


def leave_out(loco, token, shape, row, height, tiles, count, labels, phen, sums):
    people = phen.shape[1]
    anywhere = pl.BlockSpec(memory_space=pl.ANY)
    specs = [anywhere, pl.BlockSpec(memory_space=pltpu.SMEM)] + [pl.BlockSpec(memory_space=VMEM)] * (1 + len(sums))
    args = [token, labels] + [pltpu.with_memory_space_constraint(a, VMEM) for a in (phen, *sums)]
    before, aliases = 1, {0: 1}
    if loco is not None:
        specs, args, before, aliases = [anywhere] + specs, [loco] + args, 2, {0: 0, 1: 1}

    def body(*refs):
        ins, (out, _, *scratch) = refs[before : len(args)], refs[len(args) :]
        loco_body(row, shape[1], tiles, count, *ins, out, *scratch)

    return pl.pallas_call(
        body,
        out_shape=[jax.ShapeDtypeStruct(shape, jnp.bfloat16), jax.ShapeDtypeStruct(token.shape, token.dtype)],
        in_specs=specs,
        out_specs=[anywhere, anywhere],
        scratch_shapes=[pltpu.VMEM((height, people), jnp.float32), pltpu.VMEM((shape[0], height, people), jnp.float32)]
        + [pltpu.VMEM((shape[0], height, people), jnp.bfloat16), pltpu.SemaphoreType.DMA((3,))],
        input_output_aliases=aliases,
        cost_estimate=pl.CostEstimate(flops=1, bytes_accessed=1, transcendentals=0),
        compiler_params=pltpu.CompilerParams(vmem_limit_bytes=8 * 2**20),
    )(*args)


def piece_steps(genotypes, estimate, phenotypes, prior_logit, slab_var, noise_var, tile_chrom):
    people_dev, mark_dev = genotypes.shape
    shard = estimate.shape[0]
    mk_count = lax.axis_size("mk")
    people_count = lax.axis_size(("pp", "sub"))
    marker_root = math.sqrt(mark_dev * mk_count)
    people_root = math.sqrt(people_dev * people_count)
    tile_dev = mark_dev // TILE
    swap = [(0, 1), (1, 0)]

    def along(step):
        return [(i, i ^ step) for i in range(mk_count)]

    firsts, row = [], 0
    for part in FIRST:
        firsts.append((row, shard * part // sum(FIRST)))
        row += firsts[-1][1]
    seconds = [(of, firsts[of][1] * a // n, firsts[of][1] * b // n - firsts[of][1] * a // n) for of, a, b, n in SECOND]

    own = []
    for (row, height), count in zip(firsts, TRAVEL):
        each = height // count
        own.append([estimate[row + at * each : row + at * each + each] for at in range(count)])
    steps, whole, loco = Steps(genotypes), None, None
    across = [[lax.ppermute(one, "pp", swap) for one in own[0]]]
    mirror = [list(ones) for ones in own]
    mirror[0][0], coefs = steps.call(
        open_body,
        [pltpu.VMEM(own[0][0].shape, estimate.dtype), pltpu.VMEM((shard, 128), jnp.float32)],
        args=[own[0][0], *[one.reshape(1, shard) for one in (prior_logit, slab_var, noise_var)]],
        touch=True,
    )
    coefs_across = lax.ppermute(coefs, "pp", swap)
    for ones in own[1:]:
        if STAGGER:
            ones[0] = steps.call(copy_body, [pltpu.VMEM(ones[0].shape, estimate.dtype)], args=ones[:1], after=across[0])[0]
        across.append([lax.ppermute(one, "pp", swap) for one in ones])
    beside = [[lax.ppermute(one, "sub", swap) for one in ones] for ones in mirror]
    corner = [[lax.ppermute(one, "sub", swap) for one in across[0]]] + [None] * (len(across) - 1)
    before, after = [{} for _ in firsts], [{} for _ in seconds]
    f32, bf16 = jnp.float32, jnp.bfloat16
    for stage, at in ORDER:
        if stage == "pass":
            shapes = [pltpu.VMEM(one.shape, one.dtype) for one in across[at]]
            corner[at] = [lax.ppermute(one, "sub", swap) for one in steps.call(copy_body, shapes, args=across[at], after=[coefs_across])]
            continue
        if stage in ("pred", "two", "res"):
            now, (row, height) = before[at], firsts[at]
        else:
            now, (of, low, height) = after[at], seconds[at]
            row = firsts[of][0] + low
        half, wide = (2 * height, people_dev), (2 * height, mark_dev)
        if stage == "pred":
            keep, send = steps.call(
                functools.partial(predict_body, len(own[at])),
                [pltpu.VMEM(half, f32), pltpu.VMEM(half, bf16)],
                args=own[at] + across[at] + beside[at] + corner[at],
                streamed=True,
                scratch=[pltpu.VMEM((4 * height, people_dev), f32)],
            )
            now["pred"] = keep, lax.ppermute(send, "mk", along(1))
        elif stage == "two":
            (two,) = steps.call(two_body, [pltpu.VMEM(half, bf16)], args=now["pred"])
            now["two"] = two, lax.ppermute(two, "mk", along(2))
        elif stage == "res":
            body = functools.partial(residual_body, shard, row)
            (residual,) = steps.call(body, [pltpu.VMEM(half, bf16)], args=[phenotypes, *now["two"]], touch=at in TOUCHED)
            now["res"] = residual, lax.ppermute(residual, "mk", along(1))
        elif stage == "score":
            keep, *sends = steps.call(
                functools.partial(score_body, low),
                [pltpu.VMEM(wide, f32)] + [pltpu.VMEM((2 * height, mark_dev // SCORE_SPLIT), bf16)] * SCORE_SPLIT,
                args=before[of]["res"],
                streamed=True,
            )
            now["score"] = [keep] + [lax.ppermute(send, "sub", swap) for send in sends]
        elif stage == "chip":
            held = [after[at - 1]["chip"][1]] if at and CROSS[at - 1] > 1 and HOLD_CHIP else []
            parts = [pltpu.VMEM((2 * height, mark_dev // CROSS[at]), bf16)] * CROSS[at]
            chip, *sends = steps.call(chip_body, [pltpu.VMEM(wide, f32), *parts], args=now["score"], after=held, reuse=REUSE)
            now["chip"] = [chip] + [lax.ppermute(send, "pp", swap) for send in sends]
        elif stage == "den":
            chip, *came = now["chip"]
            shares = DENOISE[at] if len(came) > 1 else (SPLIT,)
            per, tiles = len(came) // len(shares), tile_dev // len(shares)
            ours, theirs = [], []
            for share, pieces in enumerate(shares):
                updated = steps.call(
                    functools.partial(denoise_body, marker_root, people_root, low, row, share * tiles, per, len(own[of])),
                    [pltpu.VMEM((2 * height, tiles * TILE // pieces), bf16)] * pieces,
                    args=[*own[of], *across[of], coefs, coefs_across, chip, *came[share * per : (share + 1) * per]],
                )
                ours += updated
                theirs += [lax.ppermute(one, "sub", swap) for one in updated]
            now["den"] = ours + theirs
        elif stage == "store":
            mine = now["den"][: len(now["den"]) // 2]
            (whole,) = steps.call(
                functools.partial(store_body, row),
                [],
                args=mine,
                scratch=[pltpu.SemaphoreType.DMA((len(mine),))],
                into=whole,
                fresh=None if whole is not None else jax.ShapeDtypeStruct(estimate.shape, estimate.dtype),
            )
        elif stage == "chrom":
            block, together = (SPAN, height, people_dev), at in TOGETHER
            pieces = len(now["den"]) // 2
            sums = steps.call(
                functools.partial(chrom_body, together, pieces),
                [pltpu.VMEM((mk_count, *block), bf16)] if together else [pltpu.VMEM(block, bf16)] * mk_count,
                [tile_chrom],
                now["den"],
                streamed=True,
                scratch=[pltpu.VMEM((4 * height, people_dev), f32)],
                after=[after[at - 1]["chrom"][3]] if at and HOLD else [],
            )
            if together:
                now["chrom"] = [lax.all_to_all(sums[0], "mk", 0, 0, tiled=True)]
            else:
                now["chrom"] = [sums[0]] + [lax.ppermute(sums[step], "mk", along(step)) for step in range(1, mk_count)]
        else:
            shape = (CHROMS, shard, people_dev)
            loco, token = leave_out(
                loco, steps.token, shape, row, height, tile_dev, mk_count, tile_chrom, phenotypes, now["chrom"]
            )
            if CHAIN:
                steps.token = token
    return (whole, loco)


def solution(mesh):
    placed = (
        P(("grp", "pp", "sub"), "mk"),
        P(("grp", "pp", "sub"), "mk"),
        P("grp", ("pp", "sub")),
        P(("grp", "pp", "sub")),
        P(("grp", "pp", "sub")),
        P(("grp", "pp", "sub")),
        P("grp"),
    )
    by_pieces = (mesh.shape["pp"], mesh.shape["sub"], mesh.shape["mk"]) == (2, 2, 4)
    return jax.shard_map(
        piece_steps if by_pieces else whole_mesh_steps,
        mesh=mesh,
        in_specs=placed,
        out_specs=(P(("grp", "pp", "sub"), "mk"), P("grp", "mk", ("pp", "sub"))),
        check_vma=False,
    )
```

```python
import functools
import math

import jax
import jax.numpy as jnp
from jax import lax
from jax.experimental import pallas as pl
from jax.experimental.pallas import tpu as pltpu
from jax.sharding import PartitionSpec as P

CHROMS = 22
TILE = 512
SPAN = 6
LOADS = 2
SPLIT = 4
SCORE_SPLIT = 8
TOGETHER = ()
CHAIN = True
RESIDENT = True
TOUCH = False
OPEN = True
REUSE = True
STAGGER = False
TOUCHED = ()
CROSS = (2, 2)
TRAVEL = (1, 1)
DENOISE = ((1, 2), (2, 2))
LIMIT = 4
HOLD = True
HOLD_CHIP = False
FIRST = (1, 1)
SECOND = ((0, 0, 1, 1), (1, 0, 1, 1))
ORDER = (('pred', 0), ('two', 0), ('pass', 1), ('pred', 1), ('res', 0), ('two', 1), ('score', 0), ('res', 1), ('chip', 0), ('score', 1), ('chip', 1), ('den', 0), ('chrom', 0), ('den', 1), ('chrom', 1), ('leave', 0), ('store', 0), ('store', 1), ('leave', 1))


def denoise(estimate, scores, prior_logit, slab_var, noise_var, marker_root, people_root):
    observed = marker_root * estimate.astype(jnp.float32) + scores * (1.0 / people_root)
    slab_col = slab_var[:, None]
    noise_col = noise_var[:, None]
    spread = slab_col + noise_col
    log_odds = (
        prior_logit[:, None]
        + 0.5 * jnp.log(noise_col / spread)
        + 0.5 * observed * observed * (1.0 / noise_col - 1.0 / spread)
    )
    posterior = jax.nn.sigmoid(log_odds) * (slab_col / spread) * observed
    return (posterior * (1.0 / marker_root)).astype(jnp.bfloat16)


def whole_mesh_steps(genotypes, estimate, phenotypes, prior_logit, slab_var, noise_var, tile_chrom):
    people_dev, mark_dev = genotypes.shape
    mk_count = lax.axis_size("mk")
    people_count = lax.axis_size(("pp", "sub"))
    traits = phenotypes.shape[0]
    partial_pred = lax.dot_general(
        lax.all_gather(estimate, ("pp", "sub"), axis=0, tiled=True),
        genotypes,
        (((1,), (1,)), ((), ())),
        preferred_element_type=jnp.float32,
    )
    share_rows = traits // mk_count
    offset = lax.axis_index("mk") * share_rows
    phen_share = lax.dynamic_slice_in_dim(phenotypes, offset, share_rows, 0).astype(jnp.float32)
    prediction = lax.psum(partial_pred, "mk")
    residual = (phenotypes.astype(jnp.float32) - prediction).astype(jnp.bfloat16)
    scores = lax.psum_scatter(
        jnp.dot(residual, genotypes, preferred_element_type=jnp.float32),
        ("pp", "sub"),
        scatter_dimension=0,
        tiled=True,
    )
    updated = denoise(
        estimate,
        scores,
        prior_logit,
        slab_var,
        noise_var,
        math.sqrt(mark_dev * mk_count),
        math.sqrt(people_dev * people_count),
    )
    tile_dev = mark_dev // TILE
    own_tiles = lax.dynamic_slice_in_dim(tile_chrom, lax.axis_index("mk") * tile_dev, tile_dev, 0)
    labels = own_tiles[0] + jnp.arange(SPAN, dtype=jnp.int32)
    member = (labels[:, None] == own_tiles[None, :]).astype(jnp.float32)
    geno_tiles = genotypes.reshape(people_dev, tile_dev, TILE)
    shard_rows = lax.all_gather(updated, ("pp", "sub"), axis=0, tiled=True)
    tile_terms = jnp.einsum(
        "kta,pta->tkp",
        shard_rows.reshape(shard_rows.shape[0], tile_dev, TILE),
        geno_tiles,
        preferred_element_type=jnp.float32,
    )
    local_sums = jnp.einsum("st,tkp->skp", member, tile_terms, precision=lax.Precision.HIGHEST)
    received = lax.all_to_all(local_sums, "mk", split_axis=1, concat_axis=0, tiled=True)
    firsts = tile_chrom.reshape(mk_count, tile_dev)[:, 0]
    sources = (firsts[:, None] + jnp.arange(SPAN, dtype=jnp.int32)[None, :]).reshape(-1)
    assign = (jnp.arange(CHROMS, dtype=jnp.int32)[:, None] == sources[None, :]).astype(jnp.float32)
    chrom_sums = jnp.einsum("cj,jkp->ckp", assign, received, precision=lax.Precision.HIGHEST)
    combined = jnp.sum(chrom_sums, axis=0)
    loco_out = (phen_share[None] - combined[None] + chrom_sums).astype(jnp.bfloat16)
    return (updated, loco_out)


VMEM = pltpu.MemorySpace.VMEM
NT = (((1,), (1,)), ((), ()))


class Steps:
    def __init__(self, genotypes):
        self.genotypes = genotypes
        self.token = jnp.zeros((8, 128), jnp.float32)

    def call(self, body, outs, scalars=(), args=(), streamed=False, scratch=(), after=(), into=None, fresh=None, touch=False, reuse=False):
        geno = self.genotypes
        tiles = geno.shape[1] // TILE
        given = streamed or TOUCH or touch
        after = list(after) + [into] * (into is not None)
        skip = 1 + len(after)
        filled = [fresh] * (fresh is not None) + [jax.ShapeDtypeStruct(one.shape, one.dtype) for one in [into] * (into is not None)]
        count = skip + len(scalars) + len(args)

        def kernel(*refs):
            ins, rest = list(refs[skip:count]), list(refs[count:])
            if given and not streamed:
                rest.pop(0)
            if streamed and RESIDENT:
                ins += [rest.pop(0), lambda tile: None]
            elif streamed:
                source = rest.pop(0)
                held, arrived = rest[1 + len(outs) : 3 + len(outs)]
                del rest[1 + len(outs) : 3 + len(outs)]
                copies = []
                for part in range(LOADS):
                    columns = pl.ds(part * geno.shape[1] // LOADS, geno.shape[1] // LOADS)
                    copies.append(pltpu.make_async_copy(source.at[:, columns], held.at[:, columns], arrived.at[part]))
                for copy in copies:
                    copy.start()

                def need(tile):
                    if tile * LOADS % tiles == 0:
                        copies[tile * LOADS // tiles].wait()

                ins += [held, need]
            body(*ins, *rest[1:])

        anywhere = pl.BlockSpec(memory_space=pl.ANY)
        stream_scratch = [pltpu.VMEM(geno.shape, geno.dtype), pltpu.SemaphoreType.DMA((LOADS,))] if streamed and not RESIDENT else []
        token, *results = pl.pallas_call(
            kernel,
            out_shape=[jax.ShapeDtypeStruct(self.token.shape, self.token.dtype), *outs, *filled],
            in_specs=[anywhere] * skip
            + [pl.BlockSpec(memory_space=pltpu.SMEM)] * len(scalars)
            + [pl.BlockSpec(memory_space=VMEM)] * len(args)
            + [pl.BlockSpec(memory_space=VMEM) if RESIDENT else anywhere] * given,
            out_specs=[anywhere] + [pl.BlockSpec(memory_space=VMEM)] * len(outs) + [anywhere] * len(filled),
            scratch_shapes=stream_scratch + list(scratch),
            input_output_aliases={0: 0}
            | ({} if into is None else {skip - 1: 1 + len(outs)})
            | ({skip + len(scalars): 1} if reuse else {}),
            cost_estimate=pl.CostEstimate(flops=1, bytes_accessed=1, transcendentals=0),
            compiler_params=pltpu.CompilerParams(vmem_limit_bytes=LIMIT * 2**20),
        )(self.token, *after, *scalars, *[pltpu.with_memory_space_constraint(a, VMEM) for a in args], *[pltpu.with_memory_space_constraint(geno, VMEM if RESIDENT else pltpu.MemorySpace.HBM)] * given)
        if CHAIN:
            self.token = token
        return results


def columns_of(tile):
    return slice(tile * TILE, (tile + 1) * TILE)


def place():
    return lax.axis_index("pp") * 2 + lax.axis_index("sub"), lax.axis_index("mk")


def row_at(start, height):
    return pl.ds(pl.multiple_of(start, 16), height)


def piece_of(refs, tile):
    for ref in refs:
        if tile < ref.shape[1] // TILE:
            return ref, columns_of(tile)
        tile -= ref.shape[1] // TILE


def copy_body(*refs):
    count = len(refs) // 2
    for source, target in zip(refs[:count], refs[count:]):
        target[...] = source[...]


def open_body(source, prior_logit, slab_var, noise_var, target, coefs):
    target[...] = source[...]
    slab, noise = slab_var[...], noise_var[...]
    spread = slab + noise
    base = prior_logit[...] + 0.5 * jnp.log(noise / spread)
    curve = 0.5 * (1.0 / noise - 1.0 / spread)
    shard = slab.shape[1]
    here = lax.broadcasted_iota(jnp.int32, (shard, shard), 0) == lax.broadcasted_iota(jnp.int32, (shard, shard), 1)
    lane = lax.broadcasted_iota(jnp.int32, coefs.shape, 1)
    value = jnp.zeros(coefs.shape, jnp.float32)
    for at, row in enumerate((base, curve, slab / spread)):
        column = jnp.sum(jnp.where(here, jnp.broadcast_to(row, here.shape), 0.0), axis=1, keepdims=True)
        value = jnp.where(lane == at, column, value)
    coefs[...] = value


def predict_body(parts, *refs):
    blocks, (geno, need, keep, send, product) = refs[: 4 * parts], refs[4 * parts :]
    odd = place()[1] % 2
    half = keep.shape[0]
    for tile in range(geno.shape[1] // TILE):
        part = columns_of(tile)
        rows = jnp.concatenate([ref[:, part] for ref in blocks], axis=0)
        need(tile)
        term = lax.dot_general(rows, geno[:, part], NT, preferred_element_type=jnp.float32)
        product[...] = term if tile == 0 else product[...] + term
    keep[...] = product[row_at(odd * half, half), :]
    send[...] = product[row_at(half - odd * half, half), :].astype(send.dtype)


def two_body(keep, came, two):
    two[...] = (keep[...] + came[...].astype(jnp.float32)).astype(two.dtype)


def residual_body(shard, low, phen, two, came, residual):
    me, depth = place()
    height = two.shape[0] // 2
    for block in range(2):
        at = slice(block * height, (block + 1) * height)
        prediction = two[at, :].astype(jnp.float32) + came[at, :].astype(jnp.float32)
        start = (me ^ (depth % 2) ^ (2 * block)) * shard + low
        measured = phen[row_at(start, height), :].astype(jnp.float32)
        residual[at, :] = (measured - prediction).astype(residual.dtype)


def score_body(low, mine, other, geno, need, keep, *sends):
    even = place()[1] % 2 == 0
    half = keep.shape[0]
    height, block = half // 2, mine.shape[0] // 2

    def rows_of(ref):
        return jnp.concatenate([ref[low : low + height], ref[block + low : block + low + height]], axis=0)

    first = jnp.where(even, rows_of(mine), rows_of(other))
    second = jnp.where(even, rows_of(other), rows_of(mine))
    rows = jnp.concatenate([first, second], axis=0)
    for tile in range(geno.shape[1] // TILE):
        part = columns_of(tile)
        need(tile)
        product = jnp.dot(rows, geno[:, part], preferred_element_type=jnp.float32)
        keep[:, part] = product[:half]
        send, inner = piece_of(sends, tile)
        send[:, inner] = product[half:].astype(send.dtype)


def chip_body(keep, *refs):
    came, chip, sends = refs[:SCORE_SPLIT], refs[SCORE_SPLIT], refs[SCORE_SPLIT + 1 :]
    height = keep.shape[0] // 2
    for tile in range(keep.shape[1] // TILE):
        part = columns_of(tile)
        ref, inner = piece_of(came, tile)
        total = keep[:, part] + ref[:, inner].astype(jnp.float32)
        chip[:, part] = total
        send, inner = piece_of(sends, tile)
        send[:height, inner] = total[height:].astype(send.dtype)
        send[height:, inner] = total[:height].astype(send.dtype)


def denoise_body(marker_root, people_root, low, first, begin, parts, pieces, *refs):
    own, across, (coefs, coefs_across, chip, *refs) = refs[:pieces], refs[pieces : 2 * pieces], refs[2 * pieces :]
    came, updated = refs[:parts], refs[parts:]
    height = updated[0].shape[0] // 2
    at = slice(low, low + height)
    coef = jnp.concatenate([coefs[first : first + height], coefs_across[first : first + height]], axis=0)
    base, curve, gain = coef[:, 0:1], coef[:, 1:2], coef[:, 2:3]
    width = updated[0].shape[1]
    for tile in range(len(updated) * width // TILE):
        part = columns_of(begin + tile)
        other, inner = piece_of(came, tile)
        scores = chip[:, part] + other[:, inner].astype(jnp.float32)
        blocks = [jnp.concatenate([ref[:, part] for ref in block], axis=0)[at] for block in (own, across)]
        estimate = jnp.concatenate(blocks, axis=0).astype(jnp.float32)
        observed = marker_root * estimate + scores * (1.0 / people_root)
        log_odds = base + curve * observed * observed
        posterior = jax.nn.sigmoid(log_odds) * gain * observed
        ref, inner = piece_of(updated, tile)
        ref[:, inner] = (posterior * (1.0 / marker_root)).astype(ref.dtype)


def store_body(first, *refs):
    *parts, whole, stored = refs
    copies, begin, height = [], 0, parts[0].shape[0] // 2
    for at, ref in enumerate(parts):
        target = whole.at[pl.ds(first, height), pl.ds(begin, ref.shape[1])]
        copies.append(pltpu.make_async_copy(ref.at[pl.ds(0, height)], target, stored.at[at]))
        copies[-1].start()
        begin += ref.shape[1]
    for copy in copies:
        copy.wait()


def chrom_body(together, pieces, labels, *refs):
    own, beside, (geno, need, *outs, acc) = refs[:pieces], refs[pieces : 2 * pieces], refs[2 * pieces :]
    if together:
        outs = [outs[0].at[to] for to in range(outs[0].shape[0])]
    me, depth = place()
    height = own[0].shape[0] // 2
    base = depth * (geno.shape[1] // TILE)
    starts = []
    for to in range(len(outs)):
        bits = me ^ to if together else me ^ depth ^ to
        starts.append(((bits % 2) * 2 + bits // 2) * height)
    for out in outs:
        out[...] = jnp.zeros(out.shape, out.dtype)
    for tile in range(geno.shape[1] // TILE):
        part = columns_of(tile)
        halves = [ref[:, inner] for ref, inner in (piece_of(own, tile), piece_of(beside, tile))]
        rows = jnp.concatenate(halves, axis=0)
        need(tile)
        product = lax.dot_general(rows, geno[:, part], NT, preferred_element_type=jnp.float32)
        if tile == 0:
            acc[...] = product
        else:
            same = (labels[base + tile] == labels[base + tile - 1]).astype(jnp.float32)
            acc[...] = acc[...] * same + product

        def put(slot=labels[base + tile] - labels[base]):
            for start, out in zip(starts, outs):
                out[slot] = acc[row_at(start, height), :].astype(out.dtype)

        if tile + 1 == geno.shape[1] // TILE:
            put()
        else:
            pl.when(labels[base + tile + 1] != labels[base + tile])(put)


def loco_body(row, shard, tiles, count, labels, phen, *refs):
    *sums, out, base, acc, stage, done = refs
    height = base.shape[0]
    _, depth = place()
    if len(sums) == 1:
        firsts, sums = [labels[step * tiles] for step in range(count)], [sums[0].at[step] for step in range(count)]
    else:
        firsts = [labels[(depth ^ step) * tiles] for step in range(count)]
    total = jnp.zeros(base.shape, jnp.float32)
    for part in sums:
        for slot in range(SPAN):
            total = total + part[slot].astype(jnp.float32)
    base[...] = phen[row_at(depth * shard + row, height), :].astype(jnp.float32) - total

    for chrom in range(CHROMS):
        acc[chrom] = base[...]
    for first, part in zip(firsts, sums):
        for slot in range(SPAN):
            chrom = jnp.minimum(first + slot, CHROMS - 1)
            acc[chrom] = acc[chrom] + part[slot].astype(jnp.float32)
    group = -(-CHROMS // done.shape[0])
    copies = []
    for chrom in range(CHROMS):
        stage[chrom] = acc[chrom].astype(stage.dtype)
        if (chrom + 1) % group == 0 or chrom + 1 == CHROMS:
            begin = chrom // group * group
            some = pl.ds(begin, chrom + 1 - begin)
            copies.append(pltpu.make_async_copy(stage.at[some], out.at[some, pl.ds(row, height)], done.at[len(copies)]))
            copies[-1].start()
    for copy in copies:
        copy.wait()


def leave_out(loco, token, shape, row, height, tiles, count, labels, phen, sums):
    people = phen.shape[1]
    anywhere = pl.BlockSpec(memory_space=pl.ANY)
    specs = [anywhere, pl.BlockSpec(memory_space=pltpu.SMEM)] + [pl.BlockSpec(memory_space=VMEM)] * (1 + len(sums))
    args = [token, labels] + [pltpu.with_memory_space_constraint(a, VMEM) for a in (phen, *sums)]
    before, aliases = 1, {0: 1}
    if loco is not None:
        specs, args, before, aliases = [anywhere] + specs, [loco] + args, 2, {0: 0, 1: 1}

    def body(*refs):
        ins, (out, _, *scratch) = refs[before : len(args)], refs[len(args) :]
        loco_body(row, shape[1], tiles, count, *ins, out, *scratch)

    return pl.pallas_call(
        body,
        out_shape=[jax.ShapeDtypeStruct(shape, jnp.bfloat16), jax.ShapeDtypeStruct(token.shape, token.dtype)],
        in_specs=specs,
        out_specs=[anywhere, anywhere],
        scratch_shapes=[pltpu.VMEM((height, people), jnp.float32), pltpu.VMEM((shape[0], height, people), jnp.float32)]
        + [pltpu.VMEM((shape[0], height, people), jnp.bfloat16), pltpu.SemaphoreType.DMA((3,))],
        input_output_aliases=aliases,
        cost_estimate=pl.CostEstimate(flops=1, bytes_accessed=1, transcendentals=0),
        compiler_params=pltpu.CompilerParams(vmem_limit_bytes=8 * 2**20),
    )(*args)


def piece_steps(genotypes, estimate, phenotypes, prior_logit, slab_var, noise_var, tile_chrom):
    people_dev, mark_dev = genotypes.shape
    shard = estimate.shape[0]
    mk_count = lax.axis_size("mk")
    people_count = lax.axis_size(("pp", "sub"))
    marker_root = math.sqrt(mark_dev * mk_count)
    people_root = math.sqrt(people_dev * people_count)
    tile_dev = mark_dev // TILE
    swap = [(0, 1), (1, 0)]

    def along(step):
        return [(i, i ^ step) for i in range(mk_count)]

    firsts, row = [], 0
    for part in FIRST:
        firsts.append((row, shard * part // sum(FIRST)))
        row += firsts[-1][1]
    seconds = [(of, firsts[of][1] * a // n, firsts[of][1] * b // n - firsts[of][1] * a // n) for of, a, b, n in SECOND]

    own = []
    for (row, height), count in zip(firsts, TRAVEL):
        each = height // count
        own.append([estimate[row + at * each : row + at * each + each] for at in range(count)])
    steps, whole, loco = Steps(genotypes), None, None
    across = [[lax.ppermute(one, "pp", swap) for one in own[0]]]
    mirror = [list(ones) for ones in own]
    mirror[0][0], coefs = steps.call(
        open_body,
        [pltpu.VMEM(own[0][0].shape, estimate.dtype), pltpu.VMEM((shard, 128), jnp.float32)],
        args=[own[0][0], *[one.reshape(1, shard) for one in (prior_logit, slab_var, noise_var)]],
        touch=True,
    )
    coefs_across = lax.ppermute(coefs, "pp", swap)
    for ones in own[1:]:
        if STAGGER:
            ones[0] = steps.call(copy_body, [pltpu.VMEM(ones[0].shape, estimate.dtype)], args=ones[:1], after=across[0])[0]
        across.append([lax.ppermute(one, "pp", swap) for one in ones])
    beside = [[lax.ppermute(one, "sub", swap) for one in ones] for ones in mirror]
    corner = [[lax.ppermute(one, "sub", swap) for one in across[0]]] + [None] * (len(across) - 1)
    before, after = [{} for _ in firsts], [{} for _ in seconds]
    f32, bf16 = jnp.float32, jnp.bfloat16
    for stage, at in ORDER:
        if stage == "pass":
            shapes = [pltpu.VMEM(one.shape, one.dtype) for one in across[at]]
            corner[at] = [lax.ppermute(one, "sub", swap) for one in steps.call(copy_body, shapes, args=across[at], after=[coefs_across])]
            continue
        if stage in ("pred", "two", "res"):
            now, (row, height) = before[at], firsts[at]
        else:
            now, (of, low, height) = after[at], seconds[at]
            row = firsts[of][0] + low
        half, wide = (2 * height, people_dev), (2 * height, mark_dev)
        if stage == "pred":
            keep, send = steps.call(
                functools.partial(predict_body, len(own[at])),
                [pltpu.VMEM(half, f32), pltpu.VMEM(half, bf16)],
                args=own[at] + across[at] + beside[at] + corner[at],
                streamed=True,
                scratch=[pltpu.VMEM((4 * height, people_dev), f32)],
            )
            now["pred"] = keep, lax.ppermute(send, "mk", along(1))
        elif stage == "two":
            (two,) = steps.call(two_body, [pltpu.VMEM(half, bf16)], args=now["pred"])
            now["two"] = two, lax.ppermute(two, "mk", along(2))
        elif stage == "res":
            body = functools.partial(residual_body, shard, row)
            (residual,) = steps.call(body, [pltpu.VMEM(half, bf16)], args=[phenotypes, *now["two"]], touch=at in TOUCHED)
            now["res"] = residual, lax.ppermute(residual, "mk", along(1))
        elif stage == "score":
            keep, *sends = steps.call(
                functools.partial(score_body, low),
                [pltpu.VMEM(wide, f32)] + [pltpu.VMEM((2 * height, mark_dev // SCORE_SPLIT), bf16)] * SCORE_SPLIT,
                args=before[of]["res"],
                streamed=True,
            )
            now["score"] = [keep] + [lax.ppermute(send, "sub", swap) for send in sends]
        elif stage == "chip":
            held = [after[at - 1]["chip"][1]] if at and CROSS[at - 1] > 1 and HOLD_CHIP else []
            parts = [pltpu.VMEM((2 * height, mark_dev // CROSS[at]), bf16)] * CROSS[at]
            chip, *sends = steps.call(chip_body, [pltpu.VMEM(wide, f32), *parts], args=now["score"], after=held, reuse=REUSE)
            now["chip"] = [chip] + [lax.ppermute(send, "pp", swap) for send in sends]
        elif stage == "den":
            chip, *came = now["chip"]
            shares = DENOISE[at] if len(came) > 1 else (SPLIT,)
            per, tiles = len(came) // len(shares), tile_dev // len(shares)
            ours, theirs = [], []
            for share, pieces in enumerate(shares):
                updated = steps.call(
                    functools.partial(denoise_body, marker_root, people_root, low, row, share * tiles, per, len(own[of])),
                    [pltpu.VMEM((2 * height, tiles * TILE // pieces), bf16)] * pieces,
                    args=[*own[of], *across[of], coefs, coefs_across, chip, *came[share * per : (share + 1) * per]],
                )
                ours += updated
                theirs += [lax.ppermute(one, "sub", swap) for one in updated]
            now["den"] = ours + theirs
        elif stage == "store":
            mine = now["den"][: len(now["den"]) // 2]
            (whole,) = steps.call(
                functools.partial(store_body, row),
                [],
                args=mine,
                scratch=[pltpu.SemaphoreType.DMA((len(mine),))],
                into=whole,
                fresh=None if whole is not None else jax.ShapeDtypeStruct(estimate.shape, estimate.dtype),
            )
        elif stage == "chrom":
            block, together = (SPAN, height, people_dev), at in TOGETHER
            pieces = len(now["den"]) // 2
            sums = steps.call(
                functools.partial(chrom_body, together, pieces),
                [pltpu.VMEM((mk_count, *block), bf16)] if together else [pltpu.VMEM(block, bf16)] * mk_count,
                [tile_chrom],
                now["den"],
                streamed=True,
                scratch=[pltpu.VMEM((4 * height, people_dev), f32)],
                after=[after[at - 1]["chrom"][3]] if at and HOLD else [],
            )
            if together:
                now["chrom"] = [lax.all_to_all(sums[0], "mk", 0, 0, tiled=True)]
            else:
                now["chrom"] = [sums[0]] + [lax.ppermute(sums[step], "mk", along(step)) for step in range(1, mk_count)]
        else:
            shape = (CHROMS, shard, people_dev)
            loco, token = leave_out(
                loco, steps.token, shape, row, height, tile_dev, mk_count, tile_chrom, phenotypes, now["chrom"]
            )
            if CHAIN:
                steps.token = token
    return (whole, loco)


def solution(mesh):
    placed = (
        P(("grp", "pp", "sub"), "mk"),
        P(("grp", "pp", "sub"), "mk"),
        P("grp", ("pp", "sub")),
        P(("grp", "pp", "sub")),
        P(("grp", "pp", "sub")),
        P(("grp", "pp", "sub")),
        P("grp"),
    )
    by_pieces = (mesh.shape["pp"], mesh.shape["sub"], mesh.shape["mk"]) == (2, 2, 4)
    return jax.shard_map(
        piece_steps if by_pieces else whole_mesh_steps,
        mesh=mesh,
        in_specs=placed,
        out_specs=(P(("grp", "pp", "sub"), "mk"), P("grp", "mk", ("pp", "sub"))),
        check_vma=False,
    )
```
